128 devices in a mesh: lat: 8 (over y_lo, z), lon: 16 (over x, y_hi, core).
Axes of the slice: x: 4, y: 4 (y_hi: 2, y_lo: 2; y = y_hi * 2 + y_lo), z: 4, core: 2. Of those that a mesh axis runs over, the one named last changes fastest.
Arguments:
- x_first: bfloat16 [192, 768, 512], P('lat', 'lon'), may hold values from -6 to 6
- x_second: bfloat16 [192, 768, 512], P('lat', 'lon'), may hold values from -6 to 6
- cotangent: bfloat16 [192, 768, 512], P('lat', 'lon'), may hold values from -6 to 6
- gain_attn: float32 [512], replicated, may hold values from 0.1 to 1.9
- gain_mlp: float32 [512], replicated, may hold values from 0.1 to 1.9
- w_qkv: bfloat16 [512, 1536], replicated, may hold values from -0.25 to 0.25
- w_out: bfloat16 [512, 512], replicated, may hold values from -0.25 to 0.25
- w_up: bfloat16 [512, 2048], replicated, may hold values from -0.25 to 0.25
- w_down: bfloat16 [2048, 512], replicated, may hold values from -0.125 to 0.125
- bias: float32 [8, 72, 72], replicated, may hold values from -2 to 300, as said below
Outputs:
- out_first: bfloat16 [192, 768, 512], P('lat', 'lon')
- grad_input: bfloat16 [192, 768, 512], P('lat', 'lon')
- grad_up: float32 [512, 2048], P(('lat', 'lon'))
- grad_down: float32 [2048, 512], P(('lat', 'lon'))
The draws below stay inside these ranges and needn't reach their ends.
Inputs may be any that keep to these rules, and one draw needn't show every extreme that they name: Relative position bias of each head within one window.
All inputs are finite; a program needn't handle non-finite values.
Results may differ from the reference program's by a relative error of at most 0.0065.
Values may be sent and summed in bfloat16 or wider, within the bound.
A program may use at most 128 MiB of HBM per device.

```python
import jax
import jax.numpy as jnp
from jax import lax

C = 512
HEADS = 8
FF = 2048
WH = 6
WW = 12
NLAT = 192
NLON = 768
N_LAT = 8
N_LON = 16


def draw_bias(key, part):
    key = jax.random.fold_in(key, 11)
    base_key, row_key, lead_key, next_key, spacing_key, strength_key = jax.random.split(key, 6)
    window_size = WH * WW
    background = jnp.clip(0.5 * jax.random.normal(base_key, (HEADS, window_size, window_size), jnp.float32), -2.0, 2.0)
    chosen = jax.random.randint(row_key, (HEADS, window_size, 1), 0, 4) == 0
    lead_col = jax.random.randint(lead_key, (HEADS, window_size, 1), 0, window_size)
    offset = jax.random.randint(next_key, (HEADS, window_size, 1), 1, window_size)
    next_col = (lead_col + offset) % window_size
    spacing = 1.0 + 2.0 * jax.random.uniform(spacing_key, (HEADS, window_size, 1), jnp.float32)
    ranking = jax.random.permutation(strength_key, HEADS).astype(jnp.float32) / max(HEADS - 1, 1)
    strength = 4.0 + 4.0 * ranking
    strength = strength.reshape(HEADS, 1, 1)
    columns = jnp.arange(window_size, dtype=jnp.int32).reshape(1, 1, window_size)
    planted = jnp.where(columns == lead_col, strength, 0.0) + jnp.where(columns == next_col, strength - spacing, 0.0)
    return jnp.where(chosen & ((columns == lead_col) | (columns == next_col)), planted, background)


def strengthened(drawn, stream_key, source, target, parts, factor):
    owner, partner = [(jnp.arange(drawn.shape[position]) // (drawn.shape[position] // parts)).reshape([-1 if axis == position else 1 for axis in range(drawn.ndim)]) for position in (source, target)]
    chosen = jax.random.permutation(stream_key, parts)[partner]
    strong = (owner == chosen) | (owner == (partner + parts // 2) % parts)
    return jnp.where(strong, factor * drawn, drawn)


def level_of(stream_key, dims, cuts, least, high):
    def one(position, parts):
        steps = jax.random.uniform(jax.random.fold_in(jax.random.fold_in(stream_key, 6), position), (parts,), jnp.float32, least / len(cuts), high / len(cuts))
        return jnp.repeat(jnp.exp(steps), dims[position] // parts).reshape((-1,) + (1,) * (len(dims) - position - 1))

    level = one(*cuts[0])
    for cut in cuts[1:]:
        level = level * one(*cut)
    return level


def gaussian(key, extent, spread, bound, cuts=(), held_as=jnp.bfloat16):
    gain = level_of(key, extent, cuts, -0.22, 0.18) if cuts else 1.0
    entries = jax.random.normal(key, extent, jnp.float32) * spread * gain
    return jnp.minimum(jnp.maximum(entries, -bound), bound).astype(held_as)


def noise_with(stream_key, shape, deviation, most, cuts, heavy, kind=jnp.bfloat16):
    values = deviation * jax.random.normal(stream_key, shape, jnp.float32)
    if cuts:
        values = values * level_of(stream_key, shape, cuts, -0.22, 0.18)
    return jnp.clip(strengthened(values, jax.random.fold_in(stream_key, 3), *heavy), -most, most).astype(kind)


def setup_inputs(seed: int = 0) -> dict:
    seeds = jax.random.split(jax.random.key(seed), 11)
    x_first = gaussian(seeds[0], (NLAT, NLON, C), 1.0, 6.0, ((0, 8), (1, 16)))
    x_second = noise_with(seeds[1], (NLAT, NLON, C), 1.0, 6.0, ((0, 8), (1, 16)), (1, 2, 16, 2.0))
    cotangent = gaussian(seeds[2], (NLAT, NLON, C), 1.0, 6.0, ((0, 8), (1, 16)))
    gain_attn = jnp.clip(1.0 + 0.18 * jax.random.normal(seeds[3], (C,), jnp.float32), 0.1, 1.9)
    gain_mlp = jnp.clip(1.0 + 0.18 * jax.random.normal(seeds[4], (C,), jnp.float32), 0.1, 1.9)
    w_qkv = gaussian(seeds[5], (C, 3 * C), C ** -0.5, 0.25)
    w_out = gaussian(seeds[6], (C, C), C ** -0.5, 0.25)
    w_up = gaussian(seeds[7], (C, FF), C ** -0.5, 0.25)
    w_down = gaussian(seeds[8], (FF, C), FF ** -0.5, 0.125)
    bias = draw_bias(jax.random.fold_in(seeds[10], 71), 0)
    return dict(x_first=x_first, x_second=x_second, cotangent=cotangent, gain_attn=gain_attn, gain_mlp=gain_mlp, w_qkv=w_qkv, w_out=w_out, w_up=w_up, w_down=w_down, bias=bias)


norm_eps = 1e-05

def normalize(values):
    widened = values.astype(jnp.float32)
    centred = widened - lax.optimization_barrier(jnp.mean(widened, axis=-1, keepdims=True))
    scale_inv = lax.rsqrt(lax.optimization_barrier(jnp.mean(centred * centred, axis=-1, keepdims=True)) + norm_eps)
    return (centred * scale_inv, scale_inv)

def gelu_value(before):
    return 0.5 * before * (1.0 + jax.scipy.special.erf(before * 0.7071067811865476))

def gelu_slope(before):
    return 0.5 * (1.0 + jax.scipy.special.erf(before * 0.7071067811865476)) + before * jnp.exp(-0.5 * before * before) * 0.3989422804014327

def attend(windows, present, bias):
    window_count, window_size, triple = windows.shape
    head_count = bias.shape[0]
    features = triple // 3
    head_size = features // head_count
    pieces = windows.astype(jnp.float32).reshape(window_count, window_size, 3, head_count, head_size)
    scores = jnp.einsum('wqhd,wkhd->whqk', pieces[:, :, 0], pieces[:, :, 1]) * head_size ** (-0.5) + bias[None]
    scores = jnp.where(present[:, None, None, :], scores, -jnp.inf)
    highest = lax.optimization_barrier(jnp.max(scores, axis=-1, keepdims=True))
    raised = jnp.exp(scores - highest)
    attention = (raised / lax.optimization_barrier(jnp.sum(raised, axis=-1, keepdims=True))).astype(jnp.bfloat16)
    blended = jnp.einsum('whqk,wkhd->wqhd', attention.astype(jnp.float32), pieces[:, :, 2])
    return blended.reshape(window_count, window_size, features).astype(jnp.bfloat16)

def mlp_backward(row_x, row_cot, gain_mlp, w_up, w_down):
    centred, scale_inv = normalize(row_x)
    normed = (centred * gain_mlp).astype(jnp.bfloat16)
    before = jnp.dot(normed, w_up, preferred_element_type=jnp.float32)
    hidden = gelu_value(before).astype(jnp.bfloat16)
    back_hidden = jnp.dot(row_cot, w_down.T, preferred_element_type=jnp.float32)
    back_before = (back_hidden * gelu_slope(before)).astype(jnp.bfloat16)
    grad_up = jnp.dot(normed.T, back_before, preferred_element_type=jnp.float32)
    grad_down = jnp.dot(hidden.T, row_cot, preferred_element_type=jnp.float32)
    back_norm = jnp.dot(back_before, w_up.T, preferred_element_type=jnp.float32) * gain_mlp
    grad_rows = row_cot.astype(jnp.float32) + scale_inv * (back_norm - lax.optimization_barrier(jnp.mean(back_norm, axis=-1, keepdims=True)) - centred * lax.optimization_barrier(jnp.mean(back_norm * centred, axis=-1, keepdims=True)))
    return (grad_rows.astype(jnp.bfloat16), grad_up, grad_down)

def reference(x_first, x_second, cotangent, gain_attn, gain_mlp, w_qkv, w_out, w_up, w_down, bias):
    nlat, nlon, features = x_first.shape
    shift_h = WH // 2
    shift_w = WW // 2
    centred, scale_inv = normalize(x_first)
    normed = (centred * gain_attn).astype(jnp.bfloat16)
    rolled = jnp.roll(normed, shift_w, axis=1)
    padded = jnp.pad(rolled, ((shift_h, shift_h), (0, 0), (0, 0)))
    band_total = nlat // WH + 1
    band_stack = padded.reshape(band_total, WH, nlon, features)
    lat_index = jnp.arange(nlat + 2 * shift_h) - shift_h
    inside = ((lat_index >= 0) & (lat_index < nlat)).reshape(band_total, WH)
    per_band = nlon // WW

    def one_band(element):
        band_rows, band_inside = element
        projected = jnp.dot(band_rows, w_qkv, preferred_element_type=jnp.float32).astype(jnp.bfloat16)
        windows = projected.reshape(WH, per_band, WW, 3 * features).transpose(1, 0, 2, 3).reshape(per_band, WH * WW, 3 * features)
        present = jnp.broadcast_to(band_inside[None, :, None], (per_band, WH, WW)).reshape(per_band, WH * WW)
        blended = attend(windows, present, bias)
        return blended.reshape(per_band, WH, WW, features).transpose(1, 0, 2, 3).reshape(WH, nlon, features)
    attended = lax.map(one_band, (band_stack, inside)).reshape(nlat + 2 * shift_h, nlon, features)
    attended = jnp.roll(attended[shift_h:shift_h + nlat], -shift_w, axis=1)

    def first_rows(element):
        row_x, row_attended = element
        residual = row_x.astype(jnp.float32) + jnp.dot(row_attended, w_out, preferred_element_type=jnp.float32)
        mid_centred, mid_scale = normalize(residual)
        normed_mid = (mid_centred * gain_mlp).astype(jnp.bfloat16)
        hidden = gelu_value(jnp.dot(normed_mid, w_up, preferred_element_type=jnp.float32)).astype(jnp.bfloat16)
        return (residual + jnp.dot(hidden, w_down, preferred_element_type=jnp.float32)).astype(jnp.bfloat16)
    out_first = lax.map(first_rows, (x_first, attended))

    def second_rows(totals, element):
        row_x, row_cot = element
        grad_rows, grad_up, grad_down = mlp_backward(row_x, row_cot, gain_mlp, w_up, w_down)
        return ((totals[0] + grad_up, totals[1] + grad_down), grad_rows)
    initial = (jnp.zeros((features, w_up.shape[1]), jnp.float32), jnp.zeros((w_up.shape[1], features), jnp.float32))
    sums, grad_input = lax.scan(second_rows, initial, (x_second, cotangent))
    devices = N_LAT * N_LON
    return (out_first, grad_input, sums[0] / devices, sums[1] / devices)
```

```python
import functools

import jax
import jax.numpy as jnp
import numpy as np
from jax import lax
from jax.experimental import pallas as pl
from jax.experimental.pallas import tpu as pltpu
from jax.sharding import PartitionSpec as P

WH = 6
WW = 12
HEADS = 8
ROWS = 24
COLS = 48
C = 512
FF = 2048
CHUNK = 512
CHUNKS = FF // CHUNK
TILE = WH * COLS
TILES = ROWS // WH
WINDOW = WH * WW
SIDE = 16
SHIFT_H = WH // 2
SHIFT_W = WW // 2
DEVICES = 128
EPS = 1e-05
MESH = pl.DeviceIdType.MESH
F32 = jnp.float32
BF16 = jnp.bfloat16
FAR = -1e30


def nn(a, b):
    return jnp.dot(a, b, preferred_element_type=F32)


def nt(a, b):
    return lax.dot_general(a, b, (((1,), (1,)), ((), ())), preferred_element_type=F32)


def window_order():
    place = np.zeros((TILE, TILE + WH * SIDE), np.float32)
    for i in range(TILE):
        w, r, c = i // WINDOW, (i % WINDOW) // WW, i % WW
        col = SHIFT_W + w * WW + c
        place[i, r * COLS + col if col < COLS else TILE + r * SIDE + col - COLS] = 1.0
    return place


def normalize(values):
    centred = values - jnp.mean(values, axis=-1, keepdims=True)
    scale = lax.rsqrt(jnp.mean(centred * centred, axis=-1, keepdims=True) + EPS)
    return centred * scale, scale


def normal_cdf(v):
    bell = jnp.exp(v * v * -0.5)
    t = 1.0 / (1.0 + jnp.abs(v) * (0.3275911 * 0.7071067811865476))
    tail = t * 0.5307027145 + -0.7265760135
    tail = tail * t + 0.7107068705
    tail = tail * t + -0.142248368
    tail = tail * t + 0.127414796
    tail = tail * t * bell
    return jnp.where(v >= 0.0, 1.0 - tail, tail), bell


def gelu(v):
    return v * normal_cdf(v)[0]


def kernel(
    comm,
    x1_hbm, x2_hbm, cot_hbm, wqkv_hbm, wout_hbm, wup_hbm, wdown_hbm,
    gain_attn, gain_mlp, bias, place, place_t,
    out_hbm, gi_hbm, gup_out, gdn_out,
    x2, cot, normed, normed_t, cot_t, back_norm, hid, bb,
    wqkv, wout, wup, wdown, biases,
    g_up, g_dn, c_up, c_dn, h_up, h_dn, a1_up, a1_dn, u1, d1, a2_up, a2_dn, u2, d2, a3_up, a3_dn,
    x1, x1_side, row_in, corner_in, out, out_side, row_back, side_back, corner_back, qkv, att,
    load_sem, store_sem, halo_send, halo_recv, back_send, back_recv,
    core_send, core_recv, s1_send, s1_recv, s2_send, s2_recv, s3_send, s3_recv,
):
    lat = lax.axis_index("lat")
    lon = lax.axis_index("lon")
    y_lo, z = lat // 4, lat % 4
    x, y_hi, core = lon // 4, (lon // 2) % 2, lon % 2
    y = y_hi * 2 + y_lo
    lat_next, lat_prev = (lat + 1) % 8, (lat + 7) % 8
    lon_next, lon_prev = (lon + 1) % 16, (lon + 15) % 16

    def core_peer():
        return (lat, lon + 1 - 2 * core)

    def x_peer(k):
        other = (x + k) % 4
        return other, (lat, other * 4 + y_hi * 2 + core)

    def z_peer(k):
        other = (z + k) % 4
        return other, (y_lo * 4 + other, lon)

    def y_peer(k):
        other = (y + k) % 4
        lo, hi = other % 2, other // 2
        return lo, hi, (lo * 4 + z, x * 4 + hi * 2 + core)

    def load(i, src, dst):
        return pltpu.make_async_copy(src, dst, load_sem.at[i])

    loads = [
        load(0, x2_hbm, x2),
        load(1, cot_hbm, cot),
        load(2, wup_hbm, wup),
        load(3, wdown_hbm, wdown),
        load(4, x1_hbm, x1.at[pl.ds(0, ROWS)]),
        load(5, wqkv_hbm, wqkv),
        load(6, wout_hbm, wout),
    ]
    for item in loads:
        item.start()

    def remote(src, dst, send, recv, device):
        return pltpu.make_async_remote_copy(
            src_ref=src, dst_ref=dst, send_sem=send, recv_sem=recv,
            device_id=device, device_id_type=MESH,
        )

    halos = [
        remote(x1_hbm.at[pl.ds(0, SHIFT_H)], row_in, halo_send.at[0], halo_recv.at[0], (lat_prev, lon)),
        remote(
            x1_hbm.at[:, pl.ds(0, SIDE)], x1_side.at[pl.ds(0, ROWS)], halo_send.at[1], halo_recv.at[1],
            (lat, lon_prev),
        ),
        remote(
            x1_hbm.at[pl.ds(0, SHIFT_H), pl.ds(0, SIDE)], corner_in, halo_send.at[2], halo_recv.at[2],
            (lat_prev, lon_prev),
        ),
    ]
    if comm:
        barrier = pltpu.get_barrier_semaphore()
        peers = [
            (lat_next, lon), (lat_prev, lon), (lat, lon_next), (lat, lon_prev),
            (lat_next, lon_next), (lat_prev, lon_prev), core_peer(),
        ]
        for k in (1, 2, 3):
            peers += [x_peer(k)[1], z_peer(k)[1], y_peer(k)[2]]
        for peer in peers:
            pl.semaphore_signal(barrier, inc=1, device_id=peer, device_id_type=MESH)
        pl.semaphore_wait(barrier, len(peers))
        for item in halos:
            item.start()

    def core_copies(j):
        other = 1 - core
        return [
            remote(g_up.at[j, other], c_up.at[j], core_send.at[j, 0], core_recv.at[j, 0], core_peer()),
            remote(g_dn.at[j, other], c_dn.at[j], core_send.at[j, 1], core_recv.at[j, 1], core_peer()),
        ]

    def first_copies(j):
        copies = []
        for k in (1, 2, 3):
            other, device = z_peer(k)
            copies.append(remote(
                h_up.at[j, :, other], a1_up.at[k - 1, j], s1_send.at[j, k - 1, 0], s1_recv.at[j, k - 1, 0], device))
            other, device = x_peer(k)
            copies.append(remote(
                h_dn.at[j, :, other], a1_dn.at[k - 1, j], s1_send.at[j, k - 1, 1], s1_recv.at[j, k - 1, 1], device))
        return copies

    def second_copies():
        copies = []
        for k in (1, 2, 3):
            other, device = x_peer(k)
            copies.append(remote(
                u1.at[:, :, other], a2_up.at[k - 1], s2_send.at[k - 1, 0], s2_recv.at[k - 1, 0], device))
            other, device = z_peer(k)
            copies.append(remote(
                d1.at[:, other], a2_dn.at[k - 1], s2_send.at[k - 1, 1], s2_recv.at[k - 1, 1], device))
        return copies

    def third_copies():
        copies = []
        for k in (1, 2, 3):
            lo, hi, device = y_peer(k)
            copies.append(remote(
                u2.at[:, lo, hi], a3_up.at[k - 1], s3_send.at[k - 1, 0], s3_recv.at[k - 1, 0], device))
            copies.append(remote(
                d2.at[lo, hi], a3_dn.at[k - 1], s3_send.at[k - 1, 1], s3_recv.at[k - 1, 1], device))
        return copies

    def core_finish(j):
        if comm:
            for item in core_copies(j):
                item.wait()
        h_up[j] = (g_up[j, core].astype(F32) + c_up[j].astype(F32)).astype(BF16).reshape(2, 4, 8, 16, 128)
        h_dn[j] = (g_dn[j, core].astype(F32) + c_dn[j].astype(F32)).astype(BF16).reshape(2, 4, 2, 16, C)
        if comm:
            for item in first_copies(j):
                item.start()

    def first_finish():
        def wait_chunk(j, carry):
            for item in first_copies(j):
                item.wait()
            return carry

        if comm:
            lax.fori_loop(0, CHUNKS, wait_chunk, 0)
        total = h_up[:, :, z].astype(F32)
        for k in range(3):
            total += a1_up[k].astype(F32)
        u1[...] = total.astype(BF16).reshape(4, 2, 4, 2, 16, 128)
        total = h_dn[:, :, x].astype(F32)
        for k in range(3):
            total += a1_dn[k].astype(F32)
        d1[...] = total.astype(BF16).reshape(2, 4, 2, 16, C)
        if comm:
            for item in second_copies():
                item.start()

    def second_finish():
        if comm:
            for item in second_copies():
                item.wait()
        total = u1[:, :, x].astype(F32)
        for k in range(3):
            total += a2_up[k].astype(F32)
        u2[...] = total.astype(BF16)
        total = d1[:, z].astype(F32)
        for k in range(3):
            total += a2_dn[k].astype(F32)
        d2[...] = total.astype(BF16)
        if comm:
            for item in third_copies():
                item.start()

    def third_finish():
        if comm:
            for item in third_copies():
                item.wait()
        total = u2[:, y_lo, y_hi].astype(F32)
        for k in range(3):
            total += a3_up[k].astype(F32)
        gup_out[...] = total * (1.0 / DEVICES)
        total = d2[y_lo, y_hi].astype(F32)
        for k in range(3):
            total += a3_dn[k].astype(F32)
        gdn_out[...] = total * (1.0 / DEVICES)

    loads[0].wait()
    loads[1].wait()

    def prepare(t, carry):
        rows = pl.ds(pl.multiple_of(t * 384, 384), 384)
        band = pl.ds(t * 8, 8)
        centred, _ = normalize(x2[band].reshape(384, C).astype(F32))
        tile = (centred * gain_mlp[...]).astype(BF16)
        normed[rows, :] = tile
        normed_t[:, rows] = tile.T
        cot_t[:, rows] = cot[band].reshape(384, C).T
        return carry

    lax.fori_loop(0, 3, prepare, 0)
    loads[2].wait()
    loads[3].wait()

    sub = lax.broadcasted_iota(jnp.int32, (64, 8, 128), 1) < 4

    def chunk_step(j, carry):
        units = pl.ds(pl.multiple_of(j * CHUNK, CHUNK), CHUNK)
        w_in = wup[:, units]
        w_back = wdown[units, :]
        for t in range(TILES):
            rows = slice(t * TILE, (t + 1) * TILE)
            before = nn(normed[rows, :], w_in)
            back_hidden = nt(cot[WH * t:WH * (t + 1)].reshape(TILE, C), w_back)
            cdf, bell = normal_cdf(before)
            hid[rows, :] = (before * cdf).astype(BF16)
            slope = cdf + before * bell * 0.3989422804014327
            back = (back_hidden * slope).astype(BF16)
            bb[rows, :] = back
            part = nt(back, w_in)
            back_norm[rows, :] = jnp.where(j == 0, part, back_norm[rows, :] + part)
        grad_up = nn(normed_t[...], bb[...])
        pieces = [grad_up[:, 128 * i:128 * (i + 1)].reshape(64, 8, 128) for i in range(4)]
        turned = [pltpu.roll(piece, 4, 1) for piece in pieces]
        for side in range(2):
            halves = []
            for i in (0, 2):
                if side == 0:
                    halves.append(jnp.where(sub, pieces[i], turned[i + 1]))
                else:
                    halves.append(jnp.where(sub, turned[i], pieces[i + 1]))
            g_up[j, side] = jnp.concatenate(halves, axis=1).astype(BF16)
        grad_down = nn(cot_t[...], hid[...]).astype(BF16).T.reshape(16, 2, 16, C)
        g_dn[j, 0] = grad_down[:, 0]
        g_dn[j, 1] = grad_down[:, 1]
        if comm:
            for item in core_copies(j):
                item.start()

        @pl.when(j >= 1)
        def _():
            core_finish(j - 1)

        return carry

    lax.fori_loop(0, CHUNKS, chunk_step, 0)

    def input_grad(t, carry):
        rows = pl.ds(pl.multiple_of(t * TILE, TILE), TILE)
        band = pl.ds(t * WH, WH)
        centred, scale = normalize(x2[band].reshape(TILE, C).astype(F32))
        back = back_norm[rows, :] * gain_mlp[...]
        mean_back = jnp.mean(back, axis=-1, keepdims=True)
        mean_both = jnp.mean(back * centred, axis=-1, keepdims=True)
        grad = cot[band].reshape(TILE, C).astype(F32) + scale * (back - mean_back - centred * mean_both)
        x2[band] = grad.astype(BF16).reshape(WH, COLS, C)
        return carry

    lax.fori_loop(0, TILES, input_grad, 0)
    store_gi = pltpu.make_async_copy(x2, gi_hbm, store_sem.at[0])
    store_gi.start()
    core_finish(CHUNKS - 1)

    loads[4].wait()
    loads[5].wait()
    loads[6].wait()
    if comm:
        for item in halos:
            item.wait()
    x1[ROWS:ROWS + SHIFT_H] = row_in[...]
    x1_side[ROWS:ROWS + SHIFT_H] = corner_in[...]
    upper_q = lax.broadcasted_iota(jnp.int32, (WINDOW, WINDOW), 0) < WINDOW // 2
    upper_k = lax.broadcasted_iota(jnp.int32, (WINDOW, WINDOW), 1) < WINDOW // 2
    split = jnp.where(upper_q == upper_k, 0.0, jnp.where(lat == 7, FAR, 0.0))
    biases[0] = bias[...]
    biases[1] = bias[...] + split[None]
    low = lax.broadcasted_iota(jnp.int32, (WINDOW, 128), 1) < 64

    def side_copy(b):
        band = pl.ds(SHIFT_H + WH * b, WH)
        return remote(
            out_side.at[band], side_back.at[band], back_send.at[b], back_recv.at[b], (lat, lon_next))

    def far_copies():
        tail = pl.ds(ROWS, SHIFT_H)
        return [
            remote(out.at[tail], row_back, back_send.at[4], back_recv.at[4], (lat_next, lon)),
            remote(out_side.at[tail], corner_back, back_send.at[5], back_recv.at[5], (lat_next, lon_next)),
        ]

    def band_step(step, carry):
        b = TILES - 1 - step
        band = pl.ds(SHIFT_H + WH * b, WH)
        cells = jnp.concatenate(
            [x1[band].reshape(TILE, C), x1_side[band].reshape(WH * SIDE, C)], axis=0)
        tokens = nn(place[...], cells)
        centred, _ = normalize(tokens)
        qkv[...] = nn((centred * gain_attn[...]).astype(BF16), wqkv[...])
        masked = jnp.where(b == TILES - 1, 1, 0)

        def window_step(w, inner):
            rows = pl.ds(pl.multiple_of(w * WINDOW, 8), WINDOW)
            for pair in range(HEADS // 2):
                lanes = slice(128 * pair, 128 * (pair + 1))
                query = (qkv[rows, 128 * pair:128 * pair + 128] * 0.125).astype(BF16)
                key = qkv[rows, C + 128 * pair:C + 128 * pair + 128]
                value = qkv[rows, 2 * C + 128 * pair:2 * C + 128 * pair + 128]
                blended = []
                for side in range(2):
                    mine = low if side == 0 else jnp.logical_not(low)
                    scores = nt(query, jnp.where(mine, key, 0.0).astype(BF16))
                    scores = scores + biases[masked, 2 * pair + side]
                    raised = jnp.exp(scores - jnp.max(scores, axis=-1, keepdims=True)).astype(BF16)
                    blended.append(nn(raised, jnp.where(mine, value, 1.0).astype(BF16)))
                sums = pltpu.roll(jnp.where(low, blended[1], blended[0]), 64, 1)
                att[rows, lanes] = jnp.where(low, blended[0], blended[1]) / sums
            return inner

        lax.fori_loop(0, TILE // WINDOW, window_step, 0)
        residual = tokens + nn(att[...].astype(BF16), wout[...])
        mid, _ = normalize(residual)
        mid = (mid * gain_mlp[...]).astype(BF16)
        total = residual
        for j in range(CHUNKS):
            units = slice(j * CHUNK, (j + 1) * CHUNK)
            hidden = gelu(nn(mid, wup[:, units])).astype(BF16)
            total = total + nn(hidden, wdown[units, :])
        cells = nn(place_t[...], total.astype(BF16)).astype(BF16)
        out[band] = cells[:TILE].reshape(WH, COLS, C)
        out_side[band] = cells[TILE:].reshape(WH, SIDE, C)
        if comm:
            side_copy(b).start()

        @pl.when(step == 0)
        def _():
            if comm:
                for item in far_copies():
                    item.start()
            first_finish()

        @pl.when(step == 1)
        def _():
            second_finish()

        @pl.when(step == 2)
        def _():
            third_finish()

        return carry

    lax.fori_loop(0, TILES, band_step, 0)
    if comm:
        for item in far_copies():
            item.wait()
        for b in range(TILES):
            side_copy(b).wait()
    inside = pl.ds(SHIFT_H, ROWS - SHIFT_H)
    out[inside, pl.ds(0, SIDE)] = out[inside, pl.ds(0, SIDE)] + side_back[inside]
    out[0:SHIFT_H] = row_back[...]
    out[0:SHIFT_H, 0:SIDE] = out[0:SHIFT_H, 0:SIDE] + corner_back[...]
    store_out = pltpu.make_async_copy(out.at[pl.ds(0, ROWS)], out_hbm, store_sem.at[1])
    store_out.start()
    store_gi.wait()
    store_out.wait()


def scratch():
    v = pltpu.VMEM
    tokens = ROWS * COLS
    ext = ROWS + SHIFT_H
    dma = pltpu.SemaphoreType.DMA
    return [
        v((ROWS, COLS, C), BF16), v((ROWS, COLS, C), BF16), v((tokens, C), BF16), v((C, tokens), BF16),
        v((C, tokens), BF16), v((tokens, C), F32), v((tokens, CHUNK), BF16), v((tokens, CHUNK), BF16),
        v((C, 3 * C), BF16), v((C, C), BF16), v((C, FF), BF16), v((FF, C), BF16),
        v((2, HEADS, WINDOW, WINDOW), F32),
        v((CHUNKS, 2, 64, 16, 128), BF16), v((CHUNKS, 2, 16, 16, C), BF16),
        v((CHUNKS, 64, 16, 128), BF16), v((CHUNKS, 16, 16, C), BF16),
        v((CHUNKS, 2, 4, 8, 16, 128), BF16), v((CHUNKS, 2, 4, 2, 16, C), BF16),
        v((3, CHUNKS, 2, 8, 16, 128), BF16), v((3, CHUNKS, 2, 2, 16, C), BF16),
        v((CHUNKS, 2, 4, 2, 16, 128), BF16), v((2, 4, 2, 16, C), BF16),
        v((3, CHUNKS, 2, 2, 16, 128), BF16), v((3, 2, 2, 16, C), BF16),
        v((CHUNKS, 2, 2, 16, 128), BF16), v((2, 2, 16, C), BF16),
        v((3, CHUNKS, 16, 128), BF16), v((3, 16, C), BF16),
        v((ext, COLS, C), BF16), v((ext, SIDE, C), BF16), v((SHIFT_H, COLS, C), BF16),
        v((SHIFT_H, SIDE, C), BF16), v((ext, COLS, C), BF16), v((ext, SIDE, C), BF16),
        v((SHIFT_H, COLS, C), BF16), v((ext, SIDE, C), BF16), v((SHIFT_H, SIDE, C), BF16),
        v((TILE, 3 * C), F32), v((TILE, C), F32),
        dma((7,)), dma((2,)), dma((3,)), dma((3,)), dma((6,)), dma((6,)),
        dma((CHUNKS, 2)), dma((CHUNKS, 2)), dma((CHUNKS, 3, 2)), dma((CHUNKS, 3, 2)),
        dma((3, 2)), dma((3, 2)), dma((3, 2)), dma((3, 2)),
    ]


def shards(comm, x_first, x_second, cotangent, gain_attn, gain_mlp, w_qkv, w_out, w_up, w_down, bias):
    place = window_order()
    anywhere = pl.BlockSpec(memory_space=pl.ANY)
    near = pl.BlockSpec(memory_space=pltpu.VMEM)
    params = dict(vmem_limit_bytes=60 * 1024 * 1024, has_side_effects=True)
    if comm:
        params["collective_id"] = 0
    out_first, grad_input, up, down = pl.pallas_call(
        functools.partial(kernel, comm),
        out_shape=(
            jax.ShapeDtypeStruct((ROWS, COLS, C), BF16),
            jax.ShapeDtypeStruct((ROWS, COLS, C), BF16),
            jax.ShapeDtypeStruct((CHUNKS, 16, 128), F32),
            jax.ShapeDtypeStruct((16, C), F32),
        ),
        in_specs=[anywhere] * 7 + [near] * 5,
        out_specs=(anywhere, anywhere, near, near),
        scratch_shapes=scratch(),
        compiler_params=pltpu.CompilerParams(**params),
        cost_estimate=pl.CostEstimate(flops=20 * 10**9, bytes_accessed=13 * 10**6, transcendentals=10**7),
        name="swin_block",
    )(
        x_first, x_second, cotangent, w_qkv, w_out, w_up, w_down,
        gain_attn.reshape(1, C), gain_mlp.reshape(1, C), bias,
        jnp.asarray(place, BF16), jnp.asarray(place.T, BF16),
    )
    up = up.reshape(4, 4, 4, 128).transpose(2, 0, 1, 3).reshape(4, FF)
    return out_first, grad_input, up, down


def solution(mesh):
    cells = P("lat", "lon", None)
    return jax.shard_map(
        functools.partial(shards, True),
        mesh=mesh,
        in_specs=(cells, cells, cells) + (P(),) * 7,
        out_specs=(cells, cells, P(("lat", "lon"), None), P(("lat", "lon"), None)),
        check_vma=False,
    )
```

```python
import functools

import jax
import jax.numpy as jnp
import numpy as np
from jax import lax
from jax.experimental import pallas as pl
from jax.experimental.pallas import tpu as pltpu
from jax.sharding import PartitionSpec as P

WH = 6
WW = 12
HEADS = 8
ROWS = 24
COLS = 48
C = 512
FF = 2048
CHUNK = 512
CHUNKS = FF // CHUNK
TILE = WH * COLS
HALF = ROWS * COLS // 2
TILES = ROWS // WH
INNER = TILES - 1
WINDOW = WH * WW
EDGE = TILES + INNER
LAST = INNER * WH + WH // 2
SIDE = 16
SHIFT_H = WH // 2
SHIFT_W = WW // 2
DEVICES = 128
EPS = 1e-05
MESH = pl.DeviceIdType.MESH
F32 = jnp.float32
BF16 = jnp.bfloat16
FAR = -1e30


def nn(a, b):
    return jnp.dot(a, b, preferred_element_type=F32)


def nt(a, b):
    return lax.dot_general(a, b, (((1,), (1,)), ((), ())), preferred_element_type=F32)


def one_hot(windows, rows, first_col, own_cols, side_cols):
    place = np.zeros((len(windows) * WINDOW, rows * (own_cols + side_cols)), np.float32)
    for n, (row, col) in enumerate(windows):
        for i in range(WINDOW):
            r, c = row + i // WW, col + i % WW
            at = r * own_cols + c - first_col if c < COLS else rows * own_cols + r * side_cols + c - COLS
            place[n * WINDOW + i, at] = 1.0
    return place


def window_orders():
    starts = [SHIFT_W + WW * w for w in range(COLS // WW)]
    return [
        one_hot([(0, col) for col in starts], WH, 0, COLS, SIDE),
        one_hot([(WH * b, starts[-1]) for b in range(INNER)], INNER * WH, COLS - SIDE, SIDE, SIDE),
        one_hot([(0, col) for col in starts[:-1]], WH, 0, COLS, 0),
    ]


def normalize(values):
    centred = values - jnp.mean(values, axis=-1, keepdims=True)
    scale = lax.rsqrt(jnp.mean(centred * centred, axis=-1, keepdims=True) + EPS)
    return centred * scale, scale


def normal_cdf(v):
    return 0.5 + 0.5 * lax.erf(v * 0.7071067811865476)


def gelu(v):
    return v * normal_cdf(v)


def kernel(
    comm,
    x1_hbm, x2_hbm, cot_hbm, wqkv_hbm, wout_hbm, wup_hbm, wdown_hbm,
    gain_attn, gain_mlp, bias, p_last, p_side, p_inner, q_last, q_side, q_inner,
    out_hbm, gi_hbm, gup_out, gdn_out,
    x2, cot, normed, normed_t, cot_t, back_norm, hid, bb,
    wqkv, wout, wup, wdown, biases,
    g_up, g_dn, c_up, c_dn, h_up, h_dn, a1_up, a1_dn, u1, d1, a2_up, a2_dn, u2, d2, a3_up, a3_dn,
    x1, x1_side, row_in, corner_in, out, out_side, row_back, side_back, corner_back, tokens, padded, wqv_t, q_t, v_t, keys, att_t,
    load_sem, store_sem, halo_send, halo_recv, back_send, back_recv,
    core_send, core_recv, s1_send, s1_recv, s2_send, s2_recv, s3_send, s3_recv,
):
    lat = lax.axis_index("lat")
    lon = lax.axis_index("lon")
    y_lo, z = lat // 4, lat % 4
    x, y_hi, core = lon // 4, (lon // 2) % 2, lon % 2
    y = y_hi * 2 + y_lo
    lat_next, lat_prev = (lat + 1) % 8, (lat + 7) % 8
    lon_next, lon_prev = (lon + 1) % 16, (lon + 15) % 16

    def core_peer():
        return (lat, lon + 1 - 2 * core)

    def x_peer(k):
        other = (x + k) % 4
        return other, (lat, other * 4 + y_hi * 2 + core)

    def z_peer(k):
        other = (z + k) % 4
        return other, (y_lo * 4 + other, lon)

    def y_peer(k):
        other = (y + k) % 4
        lo, hi = other % 2, other // 2
        return lo, hi, (lo * 4 + z, x * 4 + hi * 2 + core)

    def load(i, src, dst):
        return pltpu.make_async_copy(src, dst, load_sem.at[i])

    loads = [
        load(0, x2_hbm, x2),
        load(1, cot_hbm, cot),
        load(2, wup_hbm, wup),
        load(3, wdown_hbm, wdown),
        load(4, x1_hbm, x1.at[pl.ds(0, ROWS)]),
        load(5, wqkv_hbm, wqkv),
        load(6, wout_hbm, wout),
    ]
    for item in loads:
        item.start()

    def remote(src, dst, send, recv, device):
        return pltpu.make_async_remote_copy(
            src_ref=src, dst_ref=dst, send_sem=send, recv_sem=recv,
            device_id=device, device_id_type=MESH,
        )

    halos = [
        remote(x1_hbm.at[pl.ds(0, SHIFT_H)], row_in, halo_send.at[0], halo_recv.at[0], (lat_prev, lon)),
        remote(
            x1_hbm.at[:, pl.ds(0, SIDE)], x1_side.at[pl.ds(0, ROWS)], halo_send.at[1], halo_recv.at[1],
            (lat, lon_prev),
        ),
        remote(
            x1_hbm.at[pl.ds(0, SHIFT_H), pl.ds(0, SIDE)], corner_in, halo_send.at[2], halo_recv.at[2],
            (lat_prev, lon_prev),
        ),
    ]
    if comm:
        barrier = pltpu.get_barrier_semaphore()
        peers = [
            (lat_next, lon), (lat_prev, lon), (lat, lon_next), (lat, lon_prev),
            (lat_next, lon_next), (lat_prev, lon_prev), core_peer(),
        ]
        for k in (1, 2, 3):
            peers += [x_peer(k)[1], z_peer(k)[1], y_peer(k)[2]]
        for peer in peers:
            pl.semaphore_signal(barrier, inc=1, device_id=peer, device_id_type=MESH)

    def meet():
        pl.semaphore_wait(barrier, len(peers))
        for item in halos:
            item.start()

    def core_copies(j):
        other = 1 - core
        return [
            remote(g_up.at[j, other], c_up.at[j], core_send.at[j, 0], core_recv.at[j, 0], core_peer()),
            remote(g_dn.at[j, other], c_dn.at[j], core_send.at[j, 1], core_recv.at[j, 1], core_peer()),
        ]

    def first_copies(j):
        copies = []
        for k in (1, 2, 3):
            other, device = z_peer(k)
            copies.append(remote(
                h_up.at[j, :, other], a1_up.at[k - 1, j], s1_send.at[j, k - 1, 0], s1_recv.at[j, k - 1, 0], device))
            other, device = x_peer(k)
            copies.append(remote(
                h_dn.at[j, :, other], a1_dn.at[k - 1, j], s1_send.at[j, k - 1, 1], s1_recv.at[j, k - 1, 1], device))
        return copies

    def second_copies():
        copies = []
        for k in (1, 2, 3):
            other, device = x_peer(k)
            copies.append(remote(
                u1.at[:, :, other], a2_up.at[k - 1], s2_send.at[k - 1, 0], s2_recv.at[k - 1, 0], device))
            other, device = z_peer(k)
            copies.append(remote(
                d1.at[:, other], a2_dn.at[k - 1], s2_send.at[k - 1, 1], s2_recv.at[k - 1, 1], device))
        return copies

    def third_copies():
        copies = []
        for k in (1, 2, 3):
            lo, hi, device = y_peer(k)
            copies.append(remote(
                u2.at[:, lo, hi], a3_up.at[k - 1], s3_send.at[k - 1, 0], s3_recv.at[k - 1, 0], device))
            copies.append(remote(
                d2.at[lo, hi], a3_dn.at[k - 1], s3_send.at[k - 1, 1], s3_recv.at[k - 1, 1], device))
        return copies

    def core_finish(j):
        if comm:
            for item in core_copies(j):
                item.wait()
        h_up[j] = (g_up[j, core].astype(F32) + c_up[j].astype(F32)).astype(BF16).reshape(2, 4, 8, 16, 128)
        h_dn[j] = (g_dn[j, core].astype(F32) + c_dn[j].astype(F32)).astype(BF16).reshape(2, 4, 2, 16, C)
        if comm:
            for item in first_copies(j):
                item.start()

    def first_finish():
        def wait_chunk(j, carry):
            for item in first_copies(j):
                item.wait()
            return carry

        if comm:
            lax.fori_loop(0, CHUNKS, wait_chunk, 0)
        total = h_up[:, :, z].astype(F32)
        for k in range(3):
            total += a1_up[k].astype(F32)
        u1[...] = total.astype(BF16).reshape(4, 2, 4, 2, 16, 128)
        total = h_dn[:, :, x].astype(F32)
        for k in range(3):
            total += a1_dn[k].astype(F32)
        d1[...] = total.astype(BF16).reshape(2, 4, 2, 16, C)
        if comm:
            for item in second_copies():
                item.start()

    def second_finish():
        if comm:
            for item in second_copies():
                item.wait()
        total = u1[:, :, x].astype(F32)
        for k in range(3):
            total += a2_up[k].astype(F32)
        u2[...] = total.astype(BF16)
        total = d1[:, z].astype(F32)
        for k in range(3):
            total += a2_dn[k].astype(F32)
        d2[...] = total.astype(BF16)
        if comm:
            for item in third_copies():
                item.start()

    def third_finish():
        if comm:
            for item in third_copies():
                item.wait()
        total = u2[:, y_lo, y_hi].astype(F32)
        for k in range(3):
            total += a3_up[k].astype(F32)
        for j in range(CHUNKS):
            for i in range(4):
                gup_out[:, CHUNK * j + 128 * i:CHUNK * j + 128 * (i + 1)] = total[j, 4 * i:4 * (i + 1)] * (1.0 / DEVICES)
        total = d2[y_lo, y_hi].astype(F32)
        for k in range(3):
            total += a3_dn[k].astype(F32)
        gdn_out[...] = total * (1.0 / DEVICES)

    loads[0].wait()
    loads[1].wait()

    def prepare(t, carry):
        rows = pl.ds(pl.multiple_of(t * 384, 384), 384)
        band = pl.ds(t * 8, 8)
        centred, _ = normalize(x2[band].reshape(384, C).astype(F32))
        tile = (centred * gain_mlp[...]).astype(BF16)
        normed[rows, :] = tile
        normed_t[:, rows] = tile.T
        cot_t[:, rows] = cot[band].reshape(384, C).T
        return carry

    lax.fori_loop(0, 3, prepare, 0)
    loads[2].wait()
    loads[3].wait()

    sub = lax.broadcasted_iota(jnp.int32, (64, 8, 128), 1) < 4

    def chunk_step(j, carry):
        units = pl.ds(pl.multiple_of(j * CHUNK, CHUNK), CHUNK)
        w_in = wup[:, units]
        w_back = wdown[units, :]
        for t in range(2):
            rows = slice(t * HALF, (t + 1) * HALF)
            before = nn(normed[rows, :], w_in)
            back_hidden = nt(cot[12 * t:12 * (t + 1)].reshape(HALF, C), w_back)
            cdf = normal_cdf(before)
            hid[rows, :] = (before * cdf).astype(BF16)
            slope = cdf + before * (jnp.exp(before * before * -0.5) * 0.3989422804014327)
            back = (back_hidden * slope).astype(BF16)
            bb[rows, :] = back
            part = nt(back, w_in)
            back_norm[rows, :] = jnp.where(j == 0, part, back_norm[rows, :] + part)
        grad_up = nn(normed_t[...], bb[...])
        pieces = [grad_up[:, 128 * i:128 * (i + 1)].reshape(64, 8, 128) for i in range(4)]
        turned = [pltpu.roll(piece, 4, 1) for piece in pieces]
        for side in range(2):
            halves = []
            for i in (0, 2):
                if side == 0:
                    halves.append(jnp.where(sub, pieces[i], turned[i + 1]))
                else:
                    halves.append(jnp.where(sub, turned[i], pieces[i + 1]))
            g_up[j, side] = jnp.concatenate(halves, axis=1).astype(BF16)
        grad_down = nn(cot_t[...], hid[...]).astype(BF16).T.reshape(16, 2, 16, C)
        g_dn[j, 0] = grad_down[:, 0]
        g_dn[j, 1] = grad_down[:, 1]
        if comm:
            pl.when(j == 0)(meet)
            for item in core_copies(j):
                item.start()

        @pl.when(j >= 1)
        def _():
            core_finish(j - 1)

        return carry

    lax.fori_loop(0, CHUNKS, chunk_step, 0)

    def input_grad(t, carry):
        rows = pl.ds(pl.multiple_of(t * TILE, TILE), TILE)
        band = pl.ds(t * WH, WH)
        centred, scale = normalize(x2[band].reshape(TILE, C).astype(F32))
        back = back_norm[rows, :] * gain_mlp[...]
        mean_back = jnp.mean(back, axis=-1, keepdims=True)
        mean_both = jnp.mean(back * centred, axis=-1, keepdims=True)
        grad = cot[band].reshape(TILE, C).astype(F32) + scale * (back - mean_back - centred * mean_both)
        x2[band] = grad.astype(BF16).reshape(WH, COLS, C)
        return carry

    lax.fori_loop(0, TILES, input_grad, 0)
    store_gi = pltpu.make_async_copy(x2, gi_hbm, store_sem.at[0])
    store_gi.start()
    core_finish(CHUNKS - 1)

    loads[4].wait()
    loads[5].wait()
    loads[6].wait()
    if comm:
        for item in halos:
            item.wait()
    x1[ROWS:ROWS + SHIFT_H] = row_in[...]
    x1_side[ROWS:ROWS + SHIFT_H] = corner_in[...]
    upper_q = lax.broadcasted_iota(jnp.int32, (WINDOW, WINDOW), 0) < WINDOW // 2
    upper_k = lax.broadcasted_iota(jnp.int32, (WINDOW, WINDOW), 1) < WINDOW // 2
    split = jnp.where(upper_q == upper_k, 0.0, jnp.where(lat == 7, FAR, 0.0))
    biases[...] = jnp.zeros(biases.shape, F32)
    for head in range(HEADS):
        lanes = pl.ds(128 * (head % 2), WINDOW)
        turned = bias[head].T
        biases[0, head // 2, :, lanes] = turned
        biases[1, head // 2, :, lanes] = turned + split
    padded[...] = jnp.zeros(padded.shape, BF16)
    wqv_t[0:C] = wqkv[:, 0:C].T
    wqv_t[C:2 * C] = wqkv[:, 2 * C:3 * C].T
    upper = lax.broadcasted_iota(jnp.int32, (128, 128), 0) < 64
    nothing = jnp.zeros((128, 128), BF16)
    gap = jnp.zeros((128 - WINDOW, 256), BF16)

    def project(windows):
        centred, _ = normalize(tokens[0:windows * WINDOW])
        centred = centred * gain_attn[...]
        for w in range(windows):
            padded[128 * w:128 * w + WINDOW] = centred[WINDOW * w:WINDOW * (w + 1)].astype(BF16)
        cells = padded[0:128 * windows]
        q_t[:, 0:128 * windows] = (nt(wqv_t[0:C], cells) * 0.125).astype(BF16)
        v_t[:, 0:128 * windows] = nt(wqv_t[C:2 * C], cells).astype(BF16)
        keys[0:128 * windows] = nn(cells, wqkv[:, C:2 * C]).astype(BF16)

    def attend(masks):
        def pair_step(pair, carry):
            heads = pl.ds(pl.multiple_of(pair * 128, 128), 128)
            for w, masked in enumerate(masks):
                cells = slice(w * 128, (w + 1) * 128)
                query = q_t[heads, cells]
                query = jnp.concatenate(
                    [jnp.where(upper, query, nothing), jnp.where(upper, nothing, query)], axis=1)
                scores = nn(keys[w * 128:w * 128 + WINDOW, heads], query) + biases[masked, pair]
                raised = jnp.exp(scores - jnp.max(scores, axis=0, keepdims=True))
                inverse = 1.0 / jnp.sum(raised, axis=0, keepdims=True)
                blended = nn(v_t[heads, cells], jnp.concatenate([raised.astype(BF16), gap], axis=0)) * inverse
                att_t[heads, cells] = jnp.where(upper, blended[:, :128], blended[:, 128:]).astype(BF16)
            return carry

        lax.fori_loop(0, HEADS // 2, pair_step, 0)

    def feed_forward(windows):
        mixed = lax.dot_general(
            att_t[:, 0:128 * windows], wout[...], (((0,), (0,)), ((), ())), preferred_element_type=F32)
        mixed = jnp.concatenate([mixed[128 * w:128 * w + WINDOW] for w in range(windows)], axis=0)
        residual = tokens[0:windows * WINDOW] + mixed
        mid, _ = normalize(residual)
        mid = (mid * gain_mlp[...]).astype(BF16)
        total = residual
        for j in range(CHUNKS):
            units = slice(j * CHUNK, (j + 1) * CHUNK)
            hidden = gelu(nn(mid, wup[:, units])).astype(BF16)
            total = total + nn(hidden, wdown[units, :])
        return total

    above = pl.ds(SHIFT_H, INNER * WH)
    last = pl.ds(LAST, WH)
    tail = pl.ds(ROWS, SHIFT_H)
    right = pl.ds(COLS - SIDE, SIDE)
    cells = jnp.concatenate([x1[last].reshape(TILE, C), x1_side[last].reshape(WH * SIDE, C)], axis=0)
    tokens[0:TILE] = nn(p_last[...], cells)
    cells = jnp.concatenate(
        [x1[above, right].reshape(INNER * WH * SIDE, C), x1_side[above].reshape(INNER * WH * SIDE, C)], axis=0)
    tokens[TILE:EDGE * WINDOW] = nn(p_side[...], cells)
    project(EDGE)
    attend([1] * TILES + [0] * INNER)
    first_finish()
    total = feed_forward(EDGE)
    cells = nn(q_last[...], total[:TILE].astype(BF16)).astype(BF16)
    out[last] = cells[:TILE].reshape(WH, COLS, C)
    out_side[last] = cells[TILE:].reshape(WH, SIDE, C)
    cells = nn(q_side[...], total[TILE:].astype(BF16)).astype(BF16)
    out[above, right] = cells[:INNER * WH * SIDE].reshape(INNER * WH, SIDE, C)
    out_side[above] = cells[INNER * WH * SIDE:].reshape(INNER * WH, SIDE, C)
    inside = pl.ds(SHIFT_H, ROWS - SHIFT_H)
    returns = [
        remote(out.at[tail], row_back, back_send.at[0], back_recv.at[0], (lat_next, lon)),
        remote(out_side.at[inside], side_back.at[inside], back_send.at[1], back_recv.at[1], (lat, lon_next)),
        remote(out_side.at[tail], corner_back, back_send.at[2], back_recv.at[2], (lat_next, lon_next)),
    ]
    if comm:
        for item in returns:
            item.start()
    second_finish()

    for b in range(INNER):
        band = pl.ds(SHIFT_H + WH * b, WH)
        rows = slice(INNER * WINDOW * b, INNER * WINDOW * (b + 1))
        tokens[rows] = nn(p_inner[...], x1[band].reshape(TILE, C))
    project(INNER * INNER)
    attend([0] * (INNER * INNER))
    third_finish()
    total = feed_forward(INNER * INNER)
    for b in range(INNER):
        band = pl.ds(SHIFT_H + WH * b, WH)
        rows = slice(INNER * WINDOW * b, INNER * WINDOW * (b + 1))
        cells = nn(q_inner[...], total[rows].astype(BF16)).astype(BF16).reshape(WH, COLS, C)
        out[band, pl.ds(0, COLS - SIDE)] = cells[:, :COLS - SIDE]
        out[band, right] = out[band, right] + cells[:, COLS - SIDE:]

    if comm:
        for item in returns:
            item.wait()
    left = pl.ds(0, SIDE)
    out[inside, left] = out[inside, left] + side_back[inside]
    out[0:SHIFT_H] = row_back[...]
    out[0:SHIFT_H, left] = out[0:SHIFT_H, left] + corner_back[...]
    store_out = pltpu.make_async_copy(out.at[pl.ds(0, ROWS)], out_hbm, store_sem.at[1])
    store_out.start()
    store_gi.wait()
    store_out.wait()


def scratch():
    v = pltpu.VMEM
    tokens = ROWS * COLS
    ext = ROWS + SHIFT_H
    wide = INNER * INNER * 128
    dma = pltpu.SemaphoreType.DMA
    return [
        v((ROWS, COLS, C), BF16), v((ROWS, COLS, C), BF16), v((tokens, C), BF16), v((C, tokens), BF16),
        v((C, tokens), BF16), v((tokens, C), F32), v((tokens, CHUNK), BF16), v((tokens, CHUNK), BF16),
        v((C, 3 * C), BF16), v((C, C), BF16), v((C, FF), BF16), v((FF, C), BF16),
        v((2, HEADS // 2, WINDOW, 256), F32),
        v((CHUNKS, 2, 64, 16, 128), BF16), v((CHUNKS, 2, 16, 16, C), BF16),
        v((CHUNKS, 64, 16, 128), BF16), v((CHUNKS, 16, 16, C), BF16),
        v((CHUNKS, 2, 4, 8, 16, 128), BF16), v((CHUNKS, 2, 4, 2, 16, C), BF16),
        v((3, CHUNKS, 2, 8, 16, 128), BF16), v((3, CHUNKS, 2, 2, 16, C), BF16),
        v((CHUNKS, 2, 4, 2, 16, 128), BF16), v((2, 4, 2, 16, C), BF16),
        v((3, CHUNKS, 2, 2, 16, 128), BF16), v((3, 2, 2, 16, C), BF16),
        v((CHUNKS, 2, 2, 16, 128), BF16), v((2, 2, 16, C), BF16),
        v((3, CHUNKS, 16, 128), BF16), v((3, 16, C), BF16),
        v((ext, COLS, C), BF16), v((ext, SIDE, C), BF16), v((SHIFT_H, COLS, C), BF16),
        v((SHIFT_H, SIDE, C), BF16), v((ext, COLS, C), BF16), v((ext, SIDE, C), BF16),
        v((SHIFT_H, COLS, C), BF16), v((ext, SIDE, C), BF16), v((SHIFT_H, SIDE, C), BF16),
        v((INNER * INNER * WINDOW, C), F32),
        v((wide, C), BF16), v((2 * C, C), BF16), v((C, wide), BF16), v((C, wide), BF16), v((wide, C), BF16), v((C, wide), BF16),
        dma((7,)), dma((2,)), dma((3,)), dma((3,)), dma((3,)), dma((3,)),
        dma((CHUNKS, 2)), dma((CHUNKS, 2)), dma((CHUNKS, 3, 2)), dma((CHUNKS, 3, 2)),
        dma((3, 2)), dma((3, 2)), dma((3, 2)), dma((3, 2)),
    ]


def shards(comm, x_first, x_second, cotangent, gain_attn, gain_mlp, w_qkv, w_out, w_up, w_down, bias):
    places = window_orders()
    anywhere = pl.BlockSpec(memory_space=pl.ANY)
    near = pl.BlockSpec(memory_space=pltpu.VMEM)
    params = dict(vmem_limit_bytes=60 * 1024 * 1024, has_side_effects=True)
    if comm:
        params["collective_id"] = 0
    out_first, grad_input, up, down = pl.pallas_call(
        functools.partial(kernel, comm),
        out_shape=(
            jax.ShapeDtypeStruct((ROWS, COLS, C), BF16),
            jax.ShapeDtypeStruct((ROWS, COLS, C), BF16),
            jax.ShapeDtypeStruct((4, FF), F32),
            jax.ShapeDtypeStruct((16, C), F32),
        ),
        in_specs=[anywhere] * 7 + [near] * 9,
        out_specs=(anywhere, anywhere, near, near),
        scratch_shapes=scratch(),
        compiler_params=pltpu.CompilerParams(**params),
        cost_estimate=pl.CostEstimate(flops=20 * 10**9, bytes_accessed=13 * 10**6, transcendentals=10**7),
        name="swin_block",
    )(
        x_first, x_second, cotangent, w_qkv, w_out, w_up, w_down,
        gain_attn.reshape(1, C), gain_mlp.reshape(1, C), bias,
        *[jnp.asarray(place, BF16) for place in places], *[jnp.asarray(place.T, BF16) for place in places],
    )
    return out_first, grad_input, up, down


def solution(mesh):
    cells = P("lat", "lon", None)
    return jax.shard_map(
        functools.partial(shards, True),
        mesh=mesh,
        in_specs=(cells, cells, cells) + (P(),) * 7,
        out_specs=(cells, cells, P(("lat", "lon"), None), P(("lat", "lon"), None)),
        check_vma=False,
    )
```

```python
import functools

import jax
import jax.numpy as jnp
import numpy as np
from jax import lax
from jax.experimental import pallas as pl
from jax.experimental.pallas import tpu as pltpu
from jax.sharding import PartitionSpec as P

WH = 6
WW = 12
HEADS = 8
ROWS = 24
COLS = 48
C = 512
FF = 2048
CHUNK = 512
CHUNKS = FF // CHUNK
TILE = WH * COLS
HALF = ROWS * COLS // 2
TILES = ROWS // WH
INNER = TILES - 1
WINDOW = WH * WW
EDGE = TILES + INNER
LAST = INNER * WH + WH // 2
SIDE = 16
SHIFT_H = WH // 2
SHIFT_W = WW // 2
DEVICES = 128
EPS = 1e-05
MESH = pl.DeviceIdType.MESH
F32 = jnp.float32
BF16 = jnp.bfloat16
FAR = -1e30


def nn(a, b):
    return jnp.dot(a, b, preferred_element_type=F32)


def nt(a, b):
    return lax.dot_general(a, b, (((1,), (1,)), ((), ())), preferred_element_type=F32)


def one_hot(windows, rows, first_col, own_cols, side_cols):
    place = np.zeros((-(-len(windows) * WINDOW // 16) * 16, rows * (own_cols + side_cols)), np.float32)
    for n, (row, col) in enumerate(windows):
        for i in range(WINDOW):
            r, c = row + i // WW, col + i % WW
            at = r * own_cols + c - first_col if c < COLS else rows * own_cols + r * side_cols + c - COLS
            place[n * WINDOW + i, at] = 1.0
    return place


def window_orders():
    starts = [SHIFT_W + WW * w for w in range(COLS // WW)]
    places = [
        one_hot([(0, col) for col in starts], WH, 0, COLS, SIDE),
        one_hot([(WH * b, starts[-1]) for b in range(INNER)], INNER * WH, COLS - SIDE, SIDE, SIDE),
        one_hot([(0, col) for col in starts[:-1]], WH, 0, COLS, 0),
    ]
    return places + [place.T[:, :count * WINDOW] for place, count in zip(places, (TILES, INNER, INNER))]


def normalize(values):
    centred = values - jnp.mean(values, axis=-1, keepdims=True)
    scale = lax.rsqrt(jnp.mean(centred * centred, axis=-1, keepdims=True) + EPS)
    return centred * scale, scale


def normal_cdf(v):
    return 0.5 + 0.5 * lax.erf(v * 0.7071067811865476)


def gelu(v):
    return v * normal_cdf(v)


def kernel(
    comm,
    x1_hbm, x2_hbm, cot_hbm, wqkv_hbm, wout_hbm, wup_hbm, wdown_hbm,
    bias_hbm, p_last_hbm, p_side_hbm, p_inner_hbm, q_last_hbm, q_side_hbm, q_inner_hbm, gain_attn, gain_mlp,
    out, gi, gup_out, gdn_out,
    x2, cot, normed, normed_t, cot_t, back_norm, hid, bb,
    wqkv, wout, wup, wdown, bias, p_last, p_side, p_inner, q_last, q_side, q_inner, biases,
    g_up, g_dn, c_up, c_dn, h_up, h_dn, a1_up, a1_dn, u1, d1, a2_up, a2_dn, u2, d2, a3_up, a3_dn,
    x1, x1_side, row_in, corner_in, out_side, row_back, side_back, corner_back, tokens, padded, wqv_t, q_t, v_t, keys, att_t,
    load_sem, halo_send, halo_recv, back_send, back_recv,
    core_send, core_recv, s1_send, s1_recv, s2_send, s2_recv, s3_send, s3_recv,
):
    lat = lax.axis_index("lat")
    lon = lax.axis_index("lon")
    y_lo, z = lat // 4, lat % 4
    x, y_hi, core = lon // 4, (lon // 2) % 2, lon % 2
    y = y_hi * 2 + y_lo
    lat_next, lat_prev = (lat + 1) % 8, (lat + 7) % 8
    lon_next, lon_prev = (lon + 1) % 16, (lon + 15) % 16

    def core_peer():
        return (lat, lon + 1 - 2 * core)

    def x_peer(k):
        other = (x + k) % 4
        return other, (lat, other * 4 + y_hi * 2 + core)

    def z_peer(k):
        other = (z + k) % 4
        return other, (y_lo * 4 + other, lon)

    def y_peer(k):
        other = (y + k) % 4
        lo, hi = other % 2, other // 2
        return lo, hi, (lo * 4 + z, x * 4 + hi * 2 + core)

    def load(i, src, dst):
        return pltpu.make_async_copy(src, dst, load_sem.at[i])

    first_loads = [load(0, x2_hbm, x2), load(1, cot_hbm, cot)]

    def weight_loads(j):
        units = pl.ds(pl.multiple_of(j * CHUNK, CHUNK), CHUNK)
        return [
            load(2 + j, wup_hbm.at[:, units], wup.at[:, units]),
            load(2 + CHUNKS + j, wdown_hbm.at[units], wdown.at[units]),
        ]

    later_loads = [
        load(2 + 2 * CHUNKS + i, src, dst)
        for i, (src, dst) in enumerate((
            (x1_hbm, x1.at[pl.ds(0, ROWS)]), (wqkv_hbm, wqkv), (wout_hbm, wout), (bias_hbm, bias),
            (p_last_hbm, p_last), (p_side_hbm, p_side), (p_inner_hbm, p_inner),
            (q_last_hbm, q_last), (q_side_hbm, q_side), (q_inner_hbm, q_inner),
        ))
    ]
    for item in first_loads + weight_loads(0):
        item.start()

    def remote(src, dst, send, recv, device):
        return pltpu.make_async_remote_copy(
            src_ref=src, dst_ref=dst, send_sem=send, recv_sem=recv,
            device_id=device, device_id_type=MESH,
        )

    halos = [
        remote(x1_hbm.at[pl.ds(0, SHIFT_H)], row_in, halo_send.at[0], halo_recv.at[0], (lat_prev, lon)),
        remote(
            x1_hbm.at[:, pl.ds(0, SIDE)], x1_side.at[pl.ds(0, ROWS)], halo_send.at[1], halo_recv.at[1],
            (lat, lon_prev),
        ),
        remote(
            x1_hbm.at[pl.ds(0, SHIFT_H), pl.ds(0, SIDE)], corner_in, halo_send.at[2], halo_recv.at[2],
            (lat_prev, lon_prev),
        ),
    ]
    if comm:
        barrier = pltpu.get_barrier_semaphore()
        peers = [
            (lat_next, lon), (lat_prev, lon), (lat, lon_next), (lat, lon_prev),
            (lat_next, lon_next), (lat_prev, lon_prev), core_peer(),
        ]
        for k in (1, 2, 3):
            peers += [x_peer(k)[1], z_peer(k)[1], y_peer(k)[2]]
        for peer in peers:
            pl.semaphore_signal(barrier, inc=1, device_id=peer, device_id_type=MESH)

    def meet():
        pl.semaphore_wait(barrier, len(peers))
        for item in halos:
            item.start()

    def core_copies(j):
        other = 1 - core
        return [
            remote(g_up.at[j, other], c_up.at[j], core_send.at[j, 0], core_recv.at[j, 0], core_peer()),
            remote(g_dn.at[j, other], c_dn.at[j], core_send.at[j, 1], core_recv.at[j, 1], core_peer()),
        ]

    def first_copies(j):
        copies = []
        for k in (1, 2, 3):
            other, device = z_peer(k)
            copies.append(remote(
                h_up.at[j, :, other], a1_up.at[k - 1, j], s1_send.at[j, k - 1, 0], s1_recv.at[j, k - 1, 0], device))
            other, device = x_peer(k)
            copies.append(remote(
                h_dn.at[j, :, other], a1_dn.at[k - 1, j], s1_send.at[j, k - 1, 1], s1_recv.at[j, k - 1, 1], device))
        return copies

    def second_copies():
        copies = []
        for k in (1, 2, 3):
            other, device = x_peer(k)
            copies.append(remote(
                u1.at[:, :, other], a2_up.at[k - 1], s2_send.at[k - 1, 0], s2_recv.at[k - 1, 0], device))
            other, device = z_peer(k)
            copies.append(remote(
                d1.at[:, other], a2_dn.at[k - 1], s2_send.at[k - 1, 1], s2_recv.at[k - 1, 1], device))
        return copies

    def third_copies():
        copies = []
        for k in (1, 2, 3):
            lo, hi, device = y_peer(k)
            copies.append(remote(
                u2.at[:, lo, hi], a3_up.at[k - 1], s3_send.at[k - 1, 0], s3_recv.at[k - 1, 0], device))
            copies.append(remote(
                d2.at[lo, hi], a3_dn.at[k - 1], s3_send.at[k - 1, 1], s3_recv.at[k - 1, 1], device))
        return copies

    def core_finish(j):
        if comm:
            for item in core_copies(j):
                item.wait()
        h_up[j] = (g_up[j, core].astype(F32) + c_up[j].astype(F32)).astype(BF16).reshape(2, 4, 8, 16, 128)
        h_dn[j] = (g_dn[j, core].astype(F32) + c_dn[j].astype(F32)).astype(BF16).reshape(2, 4, 2, 16, C)
        if comm:
            for item in first_copies(j):
                item.start()

    def first_finish():
        def wait_chunk(j, carry):
            for item in first_copies(j):
                item.wait()
            return carry

        if comm:
            lax.fori_loop(0, CHUNKS, wait_chunk, 0)
        total = h_up[:, :, z].astype(F32)
        for k in range(3):
            total += a1_up[k].astype(F32)
        u1[...] = total.astype(BF16).reshape(4, 2, 4, 2, 16, 128)
        total = h_dn[:, :, x].astype(F32)
        for k in range(3):
            total += a1_dn[k].astype(F32)
        d1[...] = total.astype(BF16).reshape(2, 4, 2, 16, C)
        if comm:
            for item in second_copies():
                item.start()

    def second_finish():
        if comm:
            for item in second_copies():
                item.wait()
        total = u1[:, :, x].astype(F32)
        for k in range(3):
            total += a2_up[k].astype(F32)
        u2[...] = total.astype(BF16)
        total = d1[:, z].astype(F32)
        for k in range(3):
            total += a2_dn[k].astype(F32)
        d2[...] = total.astype(BF16)
        if comm:
            for item in third_copies():
                item.start()

    def third_finish():
        if comm:
            for item in third_copies():
                item.wait()
        total = u2[:, y_lo, y_hi].astype(F32)
        for k in range(3):
            total += a3_up[k].astype(F32)
        for j in range(CHUNKS):
            for i in range(4):
                gup_out[:, CHUNK * j + 128 * i:CHUNK * j + 128 * (i + 1)] = total[j, 4 * i:4 * (i + 1)] * (1.0 / DEVICES)
        total = d2[y_lo, y_hi].astype(F32)
        for k in range(3):
            total += a3_dn[k].astype(F32)
        gdn_out[...] = total * (1.0 / DEVICES)

    for item in first_loads:
        item.wait()
    for j in range(1, CHUNKS):
        for item in weight_loads(j):
            item.start()

    def prepare(t, carry):
        rows = pl.ds(pl.multiple_of(t * 384, 384), 384)
        band = pl.ds(t * 8, 8)
        centred, _ = normalize(x2[band].reshape(384, C).astype(F32))
        tile = (centred * gain_mlp[...]).astype(BF16)
        normed[rows, :] = tile
        normed_t[:, rows] = tile.T
        cot_t[:, rows] = cot[band].reshape(384, C).T
        return carry

    lax.fori_loop(0, 3, prepare, 0)

    sub = lax.broadcasted_iota(jnp.int32, (64, 8, 128), 1) < 4

    def chunk_step(j, carry):
        units = pl.ds(pl.multiple_of(j * CHUNK, CHUNK), CHUNK)
        for item in weight_loads(j):
            item.wait()

        @pl.when(j == 0)
        def _():
            for item in later_loads:
                item.start()

        w_in = wup[:, units]
        w_back = wdown[units, :]
        for t in range(2):
            rows = slice(t * HALF, (t + 1) * HALF)
            before = nn(normed[rows, :], w_in)
            back_hidden = nt(cot[12 * t:12 * (t + 1)].reshape(HALF, C), w_back)
            cdf = normal_cdf(before)
            hid[rows, :] = (before * cdf).astype(BF16)
            slope = cdf + before * (jnp.exp(before * before * -0.5) * 0.3989422804014327)
            back = (back_hidden * slope).astype(BF16)
            bb[rows, :] = back
            part = nt(back, w_in)
            back_norm[rows, :] = jnp.where(j == 0, part, back_norm[rows, :] + part)
        grad_up = nn(normed_t[...], bb[...])
        pieces = [grad_up[:, 128 * i:128 * (i + 1)].reshape(64, 8, 128) for i in range(4)]
        turned = [pltpu.roll(piece, 4, 1) for piece in pieces]
        for side in range(2):
            halves = []
            for i in (0, 2):
                if side == 0:
                    halves.append(jnp.where(sub, pieces[i], turned[i + 1]))
                else:
                    halves.append(jnp.where(sub, turned[i], pieces[i + 1]))
            g_up[j, side] = jnp.concatenate(halves, axis=1).astype(BF16)
        grad_down = nn(cot_t[...], hid[...]).astype(BF16).T.reshape(16, 2, 16, C)
        g_dn[j, 0] = grad_down[:, 0]
        g_dn[j, 1] = grad_down[:, 1]
        if comm:
            pl.when(j == 0)(meet)
            for item in core_copies(j):
                item.start()

        @pl.when(j >= 1)
        def _():
            core_finish(j - 1)

        return carry

    lax.fori_loop(0, CHUNKS, chunk_step, 0)

    def input_grad(t, carry):
        rows = pl.ds(pl.multiple_of(t * TILE, TILE), TILE)
        band = pl.ds(t * WH, WH)
        centred, scale = normalize(x2[band].reshape(TILE, C).astype(F32))
        back = back_norm[rows, :] * gain_mlp[...]
        mean_back = jnp.mean(back, axis=-1, keepdims=True)
        mean_both = jnp.mean(back * centred, axis=-1, keepdims=True)
        grad = cot[band].reshape(TILE, C).astype(F32) + scale * (back - mean_back - centred * mean_both)
        gi[band] = grad.astype(BF16).reshape(WH, COLS, C)
        return carry

    lax.fori_loop(0, TILES, input_grad, 0)
    core_finish(CHUNKS - 1)

    for item in later_loads:
        item.wait()
    if comm:
        for item in halos:
            item.wait()
    x1[ROWS:ROWS + SHIFT_H] = row_in[...]
    x1_side[ROWS:ROWS + SHIFT_H] = corner_in[...]
    upper_q = lax.broadcasted_iota(jnp.int32, (WINDOW, WINDOW), 0) < WINDOW // 2
    upper_k = lax.broadcasted_iota(jnp.int32, (WINDOW, WINDOW), 1) < WINDOW // 2
    split = jnp.where(upper_q == upper_k, 0.0, jnp.where(lat == 7, FAR, 0.0))
    biases[...] = jnp.zeros(biases.shape, F32)
    for head in range(HEADS):
        lanes = pl.ds(128 * (head % 2), WINDOW)
        turned = bias[head].T
        biases[0, head // 2, :, lanes] = turned
        biases[1, head // 2, :, lanes] = turned + split
    padded[...] = jnp.zeros(padded.shape, BF16)
    wqv_t[0:C] = wqkv[:, 0:C].T
    wqv_t[C:2 * C] = wqkv[:, 2 * C:3 * C].T
    upper = lax.broadcasted_iota(jnp.int32, (128, 128), 0) < 64
    nothing = jnp.zeros((128, 128), BF16)
    gap = jnp.zeros((128 - WINDOW, 256), BF16)

    def project(windows):
        centred, _ = normalize(tokens[0:windows * WINDOW])
        centred = centred * gain_attn[...]
        for w in range(windows):
            padded[128 * w:128 * w + WINDOW] = centred[WINDOW * w:WINDOW * (w + 1)].astype(BF16)
        cells = padded[0:128 * windows]
        q_t[:, 0:128 * windows] = (nt(wqv_t[0:C], cells) * 0.125).astype(BF16)
        v_t[:, 0:128 * windows] = nt(wqv_t[C:2 * C], cells).astype(BF16)
        keys[0:128 * windows] = nn(cells, wqkv[:, C:2 * C]).astype(BF16)

    def attend(masks):
        def pair_step(pair, carry):
            heads = pl.ds(pl.multiple_of(pair * 128, 128), 128)
            for w, masked in enumerate(masks):
                cells = slice(w * 128, (w + 1) * 128)
                query = q_t[heads, cells]
                query = jnp.concatenate(
                    [jnp.where(upper, query, nothing), jnp.where(upper, nothing, query)], axis=1)
                scores = nn(keys[w * 128:w * 128 + WINDOW, heads], query) + biases[masked, pair]
                raised = jnp.exp(scores - jnp.max(scores, axis=0, keepdims=True))
                inverse = 1.0 / jnp.sum(raised, axis=0, keepdims=True)
                blended = nn(v_t[heads, cells], jnp.concatenate([raised.astype(BF16), gap], axis=0)) * inverse
                att_t[heads, cells] = jnp.where(upper, blended[:, :128], blended[:, 128:]).astype(BF16)
            return carry

        lax.fori_loop(0, HEADS // 2, pair_step, 0)

    def feed_forward(windows):
        mixed = lax.dot_general(
            att_t[:, 0:128 * windows], wout[...], (((0,), (0,)), ((), ())), preferred_element_type=F32)
        mixed = jnp.concatenate([mixed[128 * w:128 * w + WINDOW] for w in range(windows)], axis=0)
        residual = tokens[0:windows * WINDOW] + mixed
        mid, _ = normalize(residual)
        mid = (mid * gain_mlp[...]).astype(BF16)
        total = residual
        for j in range(CHUNKS):
            units = slice(j * CHUNK, (j + 1) * CHUNK)
            hidden = gelu(nn(mid, wup[:, units])).astype(BF16)
            total = total + nn(hidden, wdown[units, :])
        return total

    above = pl.ds(SHIFT_H, INNER * WH)
    last = pl.ds(LAST, WH)
    tail = pl.ds(ROWS, SHIFT_H)
    right = pl.ds(COLS - SIDE, SIDE)
    cells = jnp.concatenate([x1[last].reshape(TILE, C), x1_side[last].reshape(WH * SIDE, C)], axis=0)
    tokens[0:TILE] = nn(p_last[...], cells)
    cells = jnp.concatenate(
        [x1[above, right].reshape(INNER * WH * SIDE, C), x1_side[above].reshape(INNER * WH * SIDE, C)], axis=0)
    tokens[TILE:EDGE * WINDOW] = nn(p_side[...], cells)[:INNER * WINDOW]
    project(EDGE)
    attend([1] * TILES + [0] * INNER)
    first_finish()
    total = feed_forward(EDGE)
    cells = nn(q_last[...], total[:TILE].astype(BF16)).astype(BF16)
    out[last] = cells[:TILE].reshape(WH, COLS, C)
    out_side[last] = cells[TILE:].reshape(WH, SIDE, C)
    cells = nn(q_side[...], total[TILE:].astype(BF16)).astype(BF16)
    out[above, right] = cells[:INNER * WH * SIDE].reshape(INNER * WH, SIDE, C)
    out_side[above] = cells[INNER * WH * SIDE:].reshape(INNER * WH, SIDE, C)
    inside = pl.ds(SHIFT_H, ROWS - SHIFT_H)
    returns = [
        remote(out.at[tail], row_back, back_send.at[0], back_recv.at[0], (lat_next, lon)),
        remote(out_side.at[inside], side_back.at[inside], back_send.at[1], back_recv.at[1], (lat, lon_next)),
        remote(out_side.at[tail], corner_back, back_send.at[2], back_recv.at[2], (lat_next, lon_next)),
    ]
    if comm:
        for item in returns:
            item.start()
    second_finish()

    for b in range(INNER):
        band = pl.ds(SHIFT_H + WH * b, WH)
        rows = slice(INNER * WINDOW * b, INNER * WINDOW * (b + 1))
        tokens[rows] = nn(p_inner[...], x1[band].reshape(TILE, C))[:INNER * WINDOW]
    project(INNER * INNER)
    attend([0] * (INNER * INNER))
    total = feed_forward(INNER * INNER)
    for b in range(INNER):
        band = pl.ds(SHIFT_H + WH * b, WH)
        rows = slice(INNER * WINDOW * b, INNER * WINDOW * (b + 1))
        cells = nn(q_inner[...], total[rows].astype(BF16)).astype(BF16).reshape(WH, COLS, C)
        out[band, pl.ds(0, COLS - SIDE)] = cells[:, :COLS - SIDE]
        out[band, right] = out[band, right] + cells[:, COLS - SIDE:]

    third_finish()
    if comm:
        for item in returns:
            item.wait()
    left = pl.ds(0, SIDE)
    out[inside, left] = out[inside, left] + side_back[inside]
    out[0:SHIFT_H] = row_back[...]
    out[0:SHIFT_H, left] = out[0:SHIFT_H, left] + corner_back[...]


def scratch():
    v = pltpu.VMEM
    tokens = ROWS * COLS
    ext = ROWS + SHIFT_H
    wide = INNER * INNER * 128
    dma = pltpu.SemaphoreType.DMA
    return [
        v((ROWS, COLS, C), BF16), v((ROWS, COLS, C), BF16), v((tokens, C), BF16), v((C, tokens), BF16),
        v((C, tokens), BF16), v((tokens, C), F32), v((tokens, CHUNK), BF16), v((tokens, CHUNK), BF16),
        v((C, 3 * C), BF16), v((C, C), BF16), v((C, FF), BF16), v((FF, C), BF16),
        v((HEADS, WINDOW, WINDOW), F32), *[v(place.shape, BF16) for place in window_orders()],
        v((2, HEADS // 2, WINDOW, 256), F32),
        v((CHUNKS, 2, 64, 16, 128), BF16), v((CHUNKS, 2, 16, 16, C), BF16),
        v((CHUNKS, 64, 16, 128), BF16), v((CHUNKS, 16, 16, C), BF16),
        v((CHUNKS, 2, 4, 8, 16, 128), BF16), v((CHUNKS, 2, 4, 2, 16, C), BF16),
        v((3, CHUNKS, 2, 8, 16, 128), BF16), v((3, CHUNKS, 2, 2, 16, C), BF16),
        v((CHUNKS, 2, 4, 2, 16, 128), BF16), v((2, 4, 2, 16, C), BF16),
        v((3, CHUNKS, 2, 2, 16, 128), BF16), v((3, 2, 2, 16, C), BF16),
        v((CHUNKS, 2, 2, 16, 128), BF16), v((2, 2, 16, C), BF16),
        v((3, CHUNKS, 16, 128), BF16), v((3, 16, C), BF16),
        v((ext, COLS, C), BF16), v((ext, SIDE, C), BF16), v((SHIFT_H, COLS, C), BF16),
        v((SHIFT_H, SIDE, C), BF16), v((ext, SIDE, C), BF16),
        v((SHIFT_H, COLS, C), BF16), v((ext, SIDE, C), BF16), v((SHIFT_H, SIDE, C), BF16),
        v((INNER * INNER * WINDOW, C), F32),
        v((wide, C), BF16), v((2 * C, C), BF16), v((C, wide), BF16), v((C, wide), BF16), v((wide, C), BF16), v((C, wide), BF16),
        dma((2 * CHUNKS + 12,)), dma((3,)), dma((3,)), dma((3,)), dma((3,)),
        dma((CHUNKS, 2)), dma((CHUNKS, 2)), dma((CHUNKS, 3, 2)), dma((CHUNKS, 3, 2)),
        dma((3, 2)), dma((3, 2)), dma((3, 2)), dma((3, 2)),
    ]


def place_results(first, grad, up, down, first_out, grad_out, up_out, down_out, sem):
    pairs = [(first.at[pl.ds(0, ROWS)], first_out), (grad, grad_out), (up, up_out), (down, down_out)]
    copies = [pltpu.make_async_copy(src, dst, sem.at[i]) for i, (src, dst) in enumerate(pairs)]
    for copy in copies:
        copy.start()
    for copy in copies:
        copy.wait()


def shards(comm, x_first, x_second, cotangent, gain_attn, gain_mlp, w_qkv, w_out, w_up, w_down, bias):
    places = window_orders()
    anywhere = pl.BlockSpec(memory_space=pl.ANY)
    near = pl.BlockSpec(memory_space=pltpu.VMEM)
    params = dict(vmem_limit_bytes=60 * 1024 * 1024, has_side_effects=True)
    if comm:
        params["collective_id"] = 0
    results = pl.pallas_call(
        functools.partial(kernel, comm),
        out_shape=(
            pltpu.VMEM((ROWS + SHIFT_H, COLS, C), BF16),
            pltpu.VMEM((ROWS, COLS, C), BF16),
            pltpu.VMEM((4, FF), F32),
            pltpu.VMEM((16, C), F32),
        ),
        in_specs=[anywhere] * 14 + [near] * 2,
        out_specs=(near,) * 4,
        scratch_shapes=scratch(),
        compiler_params=pltpu.CompilerParams(**params),
        cost_estimate=pl.CostEstimate(flops=20 * 10**9, bytes_accessed=13 * 10**6, transcendentals=10**7),
        name="swin_block",
    )(
        x_first, x_second, cotangent, w_qkv, w_out, w_up, w_down,
        bias, *[jnp.asarray(place, BF16) for place in places],
        gain_attn.reshape(1, C), gain_mlp.reshape(1, C),
    )
    return pl.pallas_call(
        place_results,
        out_shape=(
            jax.ShapeDtypeStruct((ROWS, COLS, C), BF16),
            jax.ShapeDtypeStruct((ROWS, COLS, C), BF16),
            jax.ShapeDtypeStruct((4, FF), F32),
            jax.ShapeDtypeStruct((16, C), F32),
        ),
        in_specs=[near] * 4,
        out_specs=(anywhere,) * 4,
        scratch_shapes=[pltpu.SemaphoreType.DMA((4,))],
        compiler_params=pltpu.CompilerParams(vmem_limit_bytes=1024 * 1024),
        name="place_results",
    )(*[pltpu.with_memory_space_constraint(item, pltpu.VMEM) for item in results])


def solution(mesh):
    cells = P("lat", "lon", None)
    return jax.shard_map(
        functools.partial(shards, True),
        mesh=mesh,
        in_specs=(cells, cells, cells) + (P(),) * 7,
        out_specs=(cells, cells, P(("lat", "lon"), None), P(("lat", "lon"), None)),
        check_vma=False,
    )
```

```python
import functools

import jax
import jax.numpy as jnp
import numpy as np
from jax import lax
from jax.experimental import pallas as pl
from jax.experimental.pallas import tpu as pltpu
from jax.sharding import PartitionSpec as P

WH = 6
WW = 12
HEADS = 8
ROWS = 24
COLS = 48
C = 512
FF = 2048
CHUNK = 512
CHUNKS = FF // CHUNK
TILE = WH * COLS
HALF = ROWS * COLS // 2
TILES = ROWS // WH
INNER = TILES - 1
WINDOW = WH * WW
EDGE = TILES + INNER
LAST = INNER * WH + WH // 2
SIDE = 16
SHIFT_H = WH // 2
SHIFT_W = WW // 2
DEVICES = 128
EPS = 1e-05
MESH = pl.DeviceIdType.MESH
F32 = jnp.float32
BF16 = jnp.bfloat16
FAR = -1e30


def nn(a, b):
    return jnp.dot(a, b, preferred_element_type=F32)


def nt(a, b):
    return lax.dot_general(a, b, (((1,), (1,)), ((), ())), preferred_element_type=F32)


def one_hot(windows, rows, first_col, own_cols, side_cols):
    place = np.zeros((-(-len(windows) * WINDOW // 16) * 16, rows * (own_cols + side_cols)), np.float32)
    for n, (row, col) in enumerate(windows):
        for i in range(WINDOW):
            r, c = row + i // WW, col + i % WW
            at = r * own_cols + c - first_col if c < COLS else rows * own_cols + r * side_cols + c - COLS
            place[n * WINDOW + i, at] = 1.0
    return place


def window_orders():
    starts = [SHIFT_W + WW * w for w in range(COLS // WW)]
    places = [
        one_hot([(0, col) for col in starts], WH, 0, COLS, SIDE),
        one_hot([(WH * b, starts[-1]) for b in range(INNER)], INNER * WH, COLS - SIDE, SIDE, SIDE),
        one_hot([(0, col) for col in starts[:-1]], WH, 0, COLS, 0),
    ]
    return places + [place.T[:, :count * WINDOW] for place, count in zip(places, (TILES, INNER, INNER))]


def normalize(values):
    centred = values - jnp.mean(values, axis=-1, keepdims=True)
    scale = lax.rsqrt(jnp.mean(centred * centred, axis=-1, keepdims=True) + EPS)
    return centred * scale, scale


def normal_cdf(v):
    return 0.5 + 0.5 * lax.erf(v * 0.7071067811865476)


def gelu(v):
    return v * normal_cdf(v)


def kernel(
    comm,
    x1_hbm, x2_hbm, cot_hbm, wqkv_hbm, wout_hbm, wup_hbm, wdown_hbm,
    bias_hbm, p_last_hbm, p_side_hbm, p_inner_hbm, q_last_hbm, q_side_hbm, q_inner_hbm, gain_attn, gain_mlp,
    out, gi, gup_out, gdn_out,
    x2, cot, normed, normed_t, cot_t, back_norm, hid, bb,
    wqkv, wout, wup, wdown, bias, p_last, p_side, p_inner, q_last, q_side, q_inner, biases,
    g_up, g_dn, c_up, c_dn, h_up, h_dn, a1_up, a1_dn, u1, d1, a2_up, a2_dn, u2, d2, a3_up, a3_dn,
    x1, x1_side, row_in, corner_in, out_side, row_back, side_back, corner_back, tokens, padded, wqv_t, q_t, v_t, keys, att_t,
    load_sem, halo_send, halo_recv, back_send, back_recv,
    core_send, core_recv, s1_send, s1_recv, s2_send, s2_recv, s3_send, s3_recv,
):
    lat = lax.axis_index("lat")
    lon = lax.axis_index("lon")
    y_lo, z = lat // 4, lat % 4
    x, y_hi, core = lon // 4, (lon // 2) % 2, lon % 2
    y = y_hi * 2 + y_lo
    lat_next, lat_prev = (lat + 1) % 8, (lat + 7) % 8
    lon_next, lon_prev = (lon + 1) % 16, (lon + 15) % 16

    def core_peer():
        return (lat, lon + 1 - 2 * core)

    def x_peer(k):
        other = (x + k) % 4
        return other, (lat, other * 4 + y_hi * 2 + core)

    def z_peer(k):
        other = (z + k) % 4
        return other, (y_lo * 4 + other, lon)

    def y_peer(k):
        other = (y + k) % 4
        lo, hi = other % 2, other // 2
        return lo, hi, (lo * 4 + z, x * 4 + hi * 2 + core)

    def load(i, src, dst):
        return pltpu.make_async_copy(src, dst, load_sem.at[i])

    first_loads = [load(0, x2_hbm, x2), load(1, cot_hbm, cot)]

    def weight_loads(j):
        units = pl.ds(pl.multiple_of(j * CHUNK, CHUNK), CHUNK)
        return [
            load(2 + j, wup_hbm.at[:, units], wup.at[:, units]),
            load(2 + CHUNKS + j, wdown_hbm.at[units], wdown.at[units]),
        ]

    later_loads = [
        load(2 + 2 * CHUNKS + i, src, dst)
        for i, (src, dst) in enumerate((
            (x1_hbm, x1.at[pl.ds(0, ROWS)]), (wqkv_hbm, wqkv), (wout_hbm, wout),
            (p_last_hbm, p_last), (p_side_hbm, p_side), (p_inner_hbm, p_inner),
            (q_last_hbm, q_last), (q_side_hbm, q_side), (q_inner_hbm, q_inner),
        ))
    ]
    bias_load = load(11 + 2 * CHUNKS, bias_hbm, bias)
    for item in [bias_load] + first_loads + weight_loads(0):
        item.start()

    def remote(src, dst, send, recv, device):
        return pltpu.make_async_remote_copy(
            src_ref=src, dst_ref=dst, send_sem=send, recv_sem=recv,
            device_id=device, device_id_type=MESH,
        )

    halos = [
        remote(x1_hbm.at[pl.ds(0, SHIFT_H)], row_in, halo_send.at[0], halo_recv.at[0], (lat_prev, lon)),
        remote(
            x1_hbm.at[:, pl.ds(0, SIDE)], x1_side.at[pl.ds(0, ROWS)], halo_send.at[1], halo_recv.at[1],
            (lat, lon_prev),
        ),
        remote(
            x1_hbm.at[pl.ds(0, SHIFT_H), pl.ds(0, SIDE)], corner_in, halo_send.at[2], halo_recv.at[2],
            (lat_prev, lon_prev),
        ),
    ]
    if comm:
        barrier = pltpu.get_barrier_semaphore()
        peers = [
            (lat_next, lon), (lat_prev, lon), (lat, lon_next), (lat, lon_prev),
            (lat_next, lon_next), (lat_prev, lon_prev), core_peer(),
        ]
        for k in (1, 2, 3):
            peers += [x_peer(k)[1], z_peer(k)[1], y_peer(k)[2]]
        for peer in peers:
            pl.semaphore_signal(barrier, inc=1, device_id=peer, device_id_type=MESH)

    def meet():
        pl.semaphore_wait(barrier, len(peers))
        for item in halos:
            item.start()

    def core_copies(j):
        other = 1 - core
        return [
            remote(g_up.at[j, other], c_up.at[j], core_send.at[j, 0], core_recv.at[j, 0], core_peer()),
            remote(g_dn.at[j, other], c_dn.at[j], core_send.at[j, 1], core_recv.at[j, 1], core_peer()),
        ]

    def first_copies(j):
        copies = []
        for k in (1, 2, 3):
            other, device = z_peer(k)
            copies.append(remote(
                h_up.at[j, :, other], a1_up.at[k - 1, j], s1_send.at[j, k - 1, 0], s1_recv.at[j, k - 1, 0], device))
            other, device = x_peer(k)
            copies.append(remote(
                h_dn.at[j, :, other], a1_dn.at[k - 1, j], s1_send.at[j, k - 1, 1], s1_recv.at[j, k - 1, 1], device))
        return copies

    def second_copies():
        copies = []
        for k in (1, 2, 3):
            other, device = x_peer(k)
            copies.append(remote(
                u1.at[:, :, other], a2_up.at[k - 1], s2_send.at[k - 1, 0], s2_recv.at[k - 1, 0], device))
            other, device = z_peer(k)
            copies.append(remote(
                d1.at[:, other], a2_dn.at[k - 1], s2_send.at[k - 1, 1], s2_recv.at[k - 1, 1], device))
        return copies

    def third_copies():
        copies = []
        for k in (1, 2, 3):
            lo, hi, device = y_peer(k)
            copies.append(remote(
                u2.at[:, lo, hi], a3_up.at[k - 1], s3_send.at[k - 1, 0], s3_recv.at[k - 1, 0], device))
            copies.append(remote(
                d2.at[lo, hi], a3_dn.at[k - 1], s3_send.at[k - 1, 1], s3_recv.at[k - 1, 1], device))
        return copies

    def core_finish(j):
        if comm:
            for item in core_copies(j):
                item.wait()
        h_up[j] = (g_up[j, core].astype(F32) + c_up[j].astype(F32)).astype(BF16).reshape(2, 4, 8, 16, 128)
        h_dn[j] = (g_dn[j, core].astype(F32) + c_dn[j].astype(F32)).astype(BF16).reshape(2, 4, 2, 16, C)
        if comm:
            for item in first_copies(j):
                item.start()

    def first_finish():
        def wait_chunk(j, carry):
            for item in first_copies(j):
                item.wait()
            return carry

        if comm:
            lax.fori_loop(0, CHUNKS, wait_chunk, 0)
        total = h_up[:, :, z].astype(F32)
        for k in range(3):
            total += a1_up[k].astype(F32)
        u1[...] = total.astype(BF16).reshape(4, 2, 4, 2, 16, 128)
        total = h_dn[:, :, x].astype(F32)
        for k in range(3):
            total += a1_dn[k].astype(F32)
        d1[...] = total.astype(BF16).reshape(2, 4, 2, 16, C)
        if comm:
            for item in second_copies():
                item.start()

    def second_finish():
        if comm:
            for item in second_copies():
                item.wait()
        total = u1[:, :, x].astype(F32)
        for k in range(3):
            total += a2_up[k].astype(F32)
        u2[...] = total.astype(BF16)
        total = d1[:, z].astype(F32)
        for k in range(3):
            total += a2_dn[k].astype(F32)
        d2[...] = total.astype(BF16)
        if comm:
            for item in third_copies():
                item.start()

    def third_finish():
        if comm:
            for item in third_copies():
                item.wait()
        total = u2[:, y_lo, y_hi].astype(F32)
        for k in range(3):
            total += a3_up[k].astype(F32)
        for j in range(CHUNKS):
            for i in range(4):
                gup_out[:, CHUNK * j + 128 * i:CHUNK * j + 128 * (i + 1)] = total[j, 4 * i:4 * (i + 1)] * (1.0 / DEVICES)
        total = d2[y_lo, y_hi].astype(F32)
        for k in range(3):
            total += a3_dn[k].astype(F32)
        gdn_out[...] = total * (1.0 / DEVICES)

    bias_load.wait()
    upper_q = lax.broadcasted_iota(jnp.int32, (WINDOW, WINDOW), 0) < WINDOW // 2
    upper_k = lax.broadcasted_iota(jnp.int32, (WINDOW, WINDOW), 1) < WINDOW // 2
    split = jnp.where(upper_q == upper_k, 0.0, jnp.where(lat == 7, FAR, 0.0))
    biases[...] = jnp.zeros(biases.shape, F32)
    for head in range(HEADS):
        lanes = pl.ds(128 * (head % 2), WINDOW)
        turned = bias[head].T
        biases[0, head // 2, :, lanes] = turned
        biases[1, head // 2, :, lanes] = turned + split
    padded[...] = jnp.zeros(padded.shape, BF16)

    for item in first_loads:
        item.wait()
    for j in range(1, CHUNKS):
        for item in weight_loads(j):
            item.start()

    def prepare(t, carry):
        rows = pl.ds(pl.multiple_of(t * 384, 384), 384)
        band = pl.ds(t * 8, 8)
        centred, _ = normalize(x2[band].reshape(384, C).astype(F32))
        tile = (centred * gain_mlp[...]).astype(BF16)
        normed[rows, :] = tile
        normed_t[:, rows] = tile.T
        cot_t[:, rows] = cot[band].reshape(384, C).T
        return carry

    lax.fori_loop(0, 3, prepare, 0)

    sub = lax.broadcasted_iota(jnp.int32, (64, 8, 128), 1) < 4

    def chunk_step(j, carry):
        units = pl.ds(pl.multiple_of(j * CHUNK, CHUNK), CHUNK)
        for item in weight_loads(j):
            item.wait()

        @pl.when(j == 0)
        def _():
            for item in later_loads:
                item.start()

        w_in = wup[:, units]
        w_back = wdown[units, :]
        for t in range(2):
            rows = slice(t * HALF, (t + 1) * HALF)
            before = nn(normed[rows, :], w_in)
            back_hidden = nt(cot[12 * t:12 * (t + 1)].reshape(HALF, C), w_back)
            cdf = normal_cdf(before)
            hid[rows, :] = (before * cdf).astype(BF16)
            slope = cdf + before * (jnp.exp(before * before * -0.5) * 0.3989422804014327)
            back = (back_hidden * slope).astype(BF16)
            bb[rows, :] = back
            part = nt(back, w_in)
            back_norm[rows, :] = jnp.where(j == 0, part, back_norm[rows, :] + part)
        grad_up = nn(normed_t[...], bb[...])
        pieces = [grad_up[:, 128 * i:128 * (i + 1)].reshape(64, 8, 128) for i in range(4)]
        turned = [pltpu.roll(piece, 4, 1) for piece in pieces]
        for side in range(2):
            halves = []
            for i in (0, 2):
                if side == 0:
                    halves.append(jnp.where(sub, pieces[i], turned[i + 1]))
                else:
                    halves.append(jnp.where(sub, turned[i], pieces[i + 1]))
            g_up[j, side] = jnp.concatenate(halves, axis=1).astype(BF16)
        grad_down = nn(cot_t[...], hid[...]).astype(BF16).T.reshape(16, 2, 16, C)
        g_dn[j, 0] = grad_down[:, 0]
        g_dn[j, 1] = grad_down[:, 1]
        if comm:
            pl.when(j == 0)(meet)
            for item in core_copies(j):
                item.start()

        @pl.when(j >= 1)
        def _():
            core_finish(j - 1)

        return carry

    lax.fori_loop(0, CHUNKS, chunk_step, 0)

    def input_grad(t, carry):
        rows = pl.ds(pl.multiple_of(t * TILE, TILE), TILE)
        band = pl.ds(t * WH, WH)
        centred, scale = normalize(x2[band].reshape(TILE, C).astype(F32))
        back = back_norm[rows, :] * gain_mlp[...]
        mean_back = jnp.mean(back, axis=-1, keepdims=True)
        mean_both = jnp.mean(back * centred, axis=-1, keepdims=True)
        grad = cot[band].reshape(TILE, C).astype(F32) + scale * (back - mean_back - centred * mean_both)
        gi[band] = grad.astype(BF16).reshape(WH, COLS, C)
        return carry

    lax.fori_loop(0, TILES, input_grad, 0)
    core_finish(CHUNKS - 1)

    for item in later_loads:
        item.wait()
    if comm:
        for item in halos:
            item.wait()
    x1[ROWS:ROWS + SHIFT_H] = row_in[...]
    x1_side[ROWS:ROWS + SHIFT_H] = corner_in[...]
    wqv_t[0:C] = wqkv[:, 0:C].T
    wqv_t[C:2 * C] = wqkv[:, 2 * C:3 * C].T
    upper = lax.broadcasted_iota(jnp.int32, (128, 128), 0) < 64
    nothing = jnp.zeros((128, 128), BF16)
    gap = jnp.zeros((128 - WINDOW, 256), BF16)

    def project(windows):
        centred, _ = normalize(tokens[0:windows * WINDOW])
        centred = centred * gain_attn[...]
        for w in range(windows):
            padded[128 * w:128 * w + WINDOW] = centred[WINDOW * w:WINDOW * (w + 1)].astype(BF16)
        cells = padded[0:128 * windows]
        q_t[:, 0:128 * windows] = (nt(wqv_t[0:C], cells) * 0.125).astype(BF16)
        v_t[:, 0:128 * windows] = nt(wqv_t[C:2 * C], cells).astype(BF16)
        keys[0:128 * windows] = nn(cells, wqkv[:, C:2 * C]).astype(BF16)

    def attend(masks):
        def pair_step(pair, carry):
            heads = pl.ds(pl.multiple_of(pair * 128, 128), 128)
            scores, weights = [], []
            for w, masked in enumerate(masks):
                query = q_t[heads, w * 128:(w + 1) * 128]
                query = jnp.concatenate(
                    [jnp.where(upper, query, nothing), jnp.where(upper, nothing, query)], axis=1)
                scores.append(nn(keys[w * 128:w * 128 + WINDOW, heads], query) + biases[masked, pair])
            for score in scores:
                raised = jnp.exp(score - jnp.max(score, axis=0, keepdims=True))
                weights.append((raised.astype(BF16), 1.0 / jnp.sum(raised, axis=0, keepdims=True)))
            for w, (raised, inverse) in enumerate(weights):
                cells = slice(w * 128, (w + 1) * 128)
                blended = nn(v_t[heads, cells], jnp.concatenate([raised, gap], axis=0)) * inverse
                att_t[heads, cells] = jnp.where(upper, blended[:, :128], blended[:, 128:]).astype(BF16)
            return carry

        lax.fori_loop(0, HEADS // 2, pair_step, 0)

    def feed_forward(windows):
        mixed = lax.dot_general(
            att_t[:, 0:128 * windows], wout[...], (((0,), (0,)), ((), ())), preferred_element_type=F32)
        mixed = jnp.concatenate([mixed[128 * w:128 * w + WINDOW] for w in range(windows)], axis=0)
        residual = tokens[0:windows * WINDOW] + mixed
        mid, _ = normalize(residual)
        mid = (mid * gain_mlp[...]).astype(BF16)
        total = residual
        units = [slice(j * CHUNK, (j + 1) * CHUNK) for j in range(CHUNKS)]
        ready = nn(mid, wup[:, units[0]])
        for j in range(CHUNKS):
            coming = nn(mid, wup[:, units[j + 1]]) if j + 1 < CHUNKS else None
            hidden = gelu(ready).astype(BF16)
            total = total + nn(hidden, wdown[units[j], :])
            ready = coming
        return total

    above = pl.ds(SHIFT_H, INNER * WH)
    last = pl.ds(LAST, WH)
    tail = pl.ds(ROWS, SHIFT_H)
    right = pl.ds(COLS - SIDE, SIDE)
    cells = jnp.concatenate([x1[last].reshape(TILE, C), x1_side[last].reshape(WH * SIDE, C)], axis=0)
    tokens[0:TILE] = nn(p_last[...], cells)
    cells = jnp.concatenate(
        [x1[above, right].reshape(INNER * WH * SIDE, C), x1_side[above].reshape(INNER * WH * SIDE, C)], axis=0)
    tokens[TILE:EDGE * WINDOW] = nn(p_side[...], cells)[:INNER * WINDOW]
    project(EDGE)
    attend([1] * TILES + [0] * INNER)
    first_finish()
    total = feed_forward(EDGE)
    cells = nn(q_last[...], total[:TILE].astype(BF16)).astype(BF16)
    out[last] = cells[:TILE].reshape(WH, COLS, C)
    out_side[last] = cells[TILE:].reshape(WH, SIDE, C)
    cells = nn(q_side[...], total[TILE:].astype(BF16)).astype(BF16)
    out[above, right] = cells[:INNER * WH * SIDE].reshape(INNER * WH, SIDE, C)
    out_side[above] = cells[INNER * WH * SIDE:].reshape(INNER * WH, SIDE, C)
    inside = pl.ds(SHIFT_H, ROWS - SHIFT_H)
    returns = [
        remote(out.at[tail], row_back, back_send.at[0], back_recv.at[0], (lat_next, lon)),
        remote(out_side.at[inside], side_back.at[inside], back_send.at[1], back_recv.at[1], (lat, lon_next)),
        remote(out_side.at[tail], corner_back, back_send.at[2], back_recv.at[2], (lat_next, lon_next)),
    ]
    if comm:
        for item in returns:
            item.start()

    for b in range(INNER):
        band = pl.ds(SHIFT_H + WH * b, WH)
        rows = slice(INNER * WINDOW * b, INNER * WINDOW * (b + 1))
        tokens[rows] = nn(p_inner[...], x1[band].reshape(TILE, C))[:INNER * WINDOW]
    project(INNER * INNER)
    second_finish()
    attend([0] * (INNER * INNER))
    total = feed_forward(INNER * INNER)
    for b in range(INNER):
        band = pl.ds(SHIFT_H + WH * b, WH)
        rows = slice(INNER * WINDOW * b, INNER * WINDOW * (b + 1))
        cells = nn(q_inner[...], total[rows].astype(BF16)).astype(BF16).reshape(WH, COLS, C)
        out[band, pl.ds(0, COLS - SIDE)] = cells[:, :COLS - SIDE]
        out[band, right] = out[band, right] + cells[:, COLS - SIDE:]

    third_finish()
    if comm:
        for item in returns:
            item.wait()
    left = pl.ds(0, SIDE)
    out[inside, left] = out[inside, left] + side_back[inside]
    out[0:SHIFT_H] = row_back[...]
    out[0:SHIFT_H, left] = out[0:SHIFT_H, left] + corner_back[...]


def scratch():
    v = pltpu.VMEM
    tokens = ROWS * COLS
    ext = ROWS + SHIFT_H
    wide = INNER * INNER * 128
    dma = pltpu.SemaphoreType.DMA
    return [
        v((ROWS, COLS, C), BF16), v((ROWS, COLS, C), BF16), v((tokens, C), BF16), v((C, tokens), BF16),
        v((C, tokens), BF16), v((tokens, C), F32), v((tokens, CHUNK), BF16), v((tokens, CHUNK), BF16),
        v((C, 3 * C), BF16), v((C, C), BF16), v((C, FF), BF16), v((FF, C), BF16),
        v((HEADS, WINDOW, WINDOW), F32), *[v(place.shape, BF16) for place in window_orders()],
        v((2, HEADS // 2, WINDOW, 256), F32),
        v((CHUNKS, 2, 64, 16, 128), BF16), v((CHUNKS, 2, 16, 16, C), BF16),
        v((CHUNKS, 64, 16, 128), BF16), v((CHUNKS, 16, 16, C), BF16),
        v((CHUNKS, 2, 4, 8, 16, 128), BF16), v((CHUNKS, 2, 4, 2, 16, C), BF16),
        v((3, CHUNKS, 2, 8, 16, 128), BF16), v((3, CHUNKS, 2, 2, 16, C), BF16),
        v((CHUNKS, 2, 4, 2, 16, 128), BF16), v((2, 4, 2, 16, C), BF16),
        v((3, CHUNKS, 2, 2, 16, 128), BF16), v((3, 2, 2, 16, C), BF16),
        v((CHUNKS, 2, 2, 16, 128), BF16), v((2, 2, 16, C), BF16),
        v((3, CHUNKS, 16, 128), BF16), v((3, 16, C), BF16),
        v((ext, COLS, C), BF16), v((ext, SIDE, C), BF16), v((SHIFT_H, COLS, C), BF16),
        v((SHIFT_H, SIDE, C), BF16), v((ext, SIDE, C), BF16),
        v((SHIFT_H, COLS, C), BF16), v((ext, SIDE, C), BF16), v((SHIFT_H, SIDE, C), BF16),
        v((INNER * INNER * WINDOW, C), F32),
        v((wide, C), BF16), v((2 * C, C), BF16), v((C, wide), BF16), v((C, wide), BF16), v((wide, C), BF16), v((C, wide), BF16),
        dma((2 * CHUNKS + 12,)), dma((3,)), dma((3,)), dma((3,)), dma((3,)),
        dma((CHUNKS, 2)), dma((CHUNKS, 2)), dma((CHUNKS, 3, 2)), dma((CHUNKS, 3, 2)),
        dma((3, 2)), dma((3, 2)), dma((3, 2)), dma((3, 2)),
    ]


def place_results(first, grad, up, down, first_out, grad_out, up_out, down_out, sem):
    pairs = [(first.at[pl.ds(0, ROWS)], first_out), (grad, grad_out), (up, up_out), (down, down_out)]
    copies = [pltpu.make_async_copy(src, dst, sem.at[i]) for i, (src, dst) in enumerate(pairs)]
    for copy in copies:
        copy.start()
    for copy in copies:
        copy.wait()


def shards(comm, x_first, x_second, cotangent, gain_attn, gain_mlp, w_qkv, w_out, w_up, w_down, bias):
    places = window_orders()
    anywhere = pl.BlockSpec(memory_space=pl.ANY)
    near = pl.BlockSpec(memory_space=pltpu.VMEM)
    params = dict(vmem_limit_bytes=60 * 1024 * 1024, has_side_effects=True)
    if comm:
        params["collective_id"] = 0
    results = pl.pallas_call(
        functools.partial(kernel, comm),
        out_shape=(
            pltpu.VMEM((ROWS + SHIFT_H, COLS, C), BF16),
            pltpu.VMEM((ROWS, COLS, C), BF16),
            pltpu.VMEM((4, FF), F32),
            pltpu.VMEM((16, C), F32),
        ),
        in_specs=[anywhere] * 14 + [near] * 2,
        out_specs=(near,) * 4,
        scratch_shapes=scratch(),
        compiler_params=pltpu.CompilerParams(**params),
        cost_estimate=pl.CostEstimate(flops=20 * 10**9, bytes_accessed=13 * 10**6, transcendentals=10**7),
        name="swin_block",
    )(
        x_first, x_second, cotangent, w_qkv, w_out, w_up, w_down,
        bias, *[jnp.asarray(place, BF16) for place in places],
        gain_attn.reshape(1, C), gain_mlp.reshape(1, C),
    )
    return pl.pallas_call(
        place_results,
        out_shape=(
            jax.ShapeDtypeStruct((ROWS, COLS, C), BF16),
            jax.ShapeDtypeStruct((ROWS, COLS, C), BF16),
            jax.ShapeDtypeStruct((4, FF), F32),
            jax.ShapeDtypeStruct((16, C), F32),
        ),
        in_specs=[near] * 4,
        out_specs=(anywhere,) * 4,
        scratch_shapes=[pltpu.SemaphoreType.DMA((4,))],
        compiler_params=pltpu.CompilerParams(vmem_limit_bytes=1024 * 1024),
        name="place_results",
    )(*[pltpu.with_memory_space_constraint(item, pltpu.VMEM) for item in results])


def solution(mesh):
    cells = P("lat", "lon", None)
    return jax.shard_map(
        functools.partial(shards, True),
        mesh=mesh,
        in_specs=(cells, cells, cells) + (P(),) * 7,
        out_specs=(cells, cells, P(("lat", "lon"), None), P(("lat", "lon"), None)),
        check_vma=False,
    )
```

```python
import functools

import jax
import jax.numpy as jnp
import numpy as np
from jax import lax
from jax.experimental import pallas as pl
from jax.experimental.pallas import tpu as pltpu
from jax.sharding import PartitionSpec as P

WH = 6
WW = 12
HEADS = 8
ROWS = 24
COLS = 48
C = 512
FF = 2048
CHUNK = 512
CHUNKS = FF // CHUNK
TILE = WH * COLS
HALF = ROWS * COLS // 2
TILES = ROWS // WH
INNER = TILES - 1
WINDOW = WH * WW
EDGE = TILES + INNER
LAST = INNER * WH + WH // 2
SIDE = 16
SHIFT_H = WH // 2
SHIFT_W = WW // 2
DEVICES = 128
EPS = 1e-05
MESH = pl.DeviceIdType.MESH
F32 = jnp.float32
BF16 = jnp.bfloat16
FAR = -1e30


def nn(a, b):
    return jnp.dot(a, b, preferred_element_type=F32)


def nt(a, b):
    return lax.dot_general(a, b, (((1,), (1,)), ((), ())), preferred_element_type=F32)


def one_hot(windows, rows, first_col, own_cols, side_cols):
    place = np.zeros((-(-len(windows) * WINDOW // 16) * 16, rows * (own_cols + side_cols)), np.float32)
    for n, (row, col) in enumerate(windows):
        for i in range(WINDOW):
            r, c = row + i // WW, col + i % WW
            at = r * own_cols + c - first_col if c < COLS else rows * own_cols + r * side_cols + c - COLS
            place[n * WINDOW + i, at] = 1.0
    return place


def window_orders():
    starts = [SHIFT_W + WW * w for w in range(COLS // WW)]
    places = [
        one_hot([(0, col) for col in starts], WH, 0, COLS, SIDE),
        one_hot([(WH * b, starts[-1]) for b in range(INNER)], INNER * WH, COLS - SIDE, SIDE, SIDE),
        one_hot([(0, col) for col in starts[:-1]], WH, 0, COLS, 0),
    ]
    return places + [place.T[:, :count * WINDOW] for place, count in zip(places, (TILES, INNER, INNER))]


def normalize(values):
    centred = values - jnp.mean(values, axis=-1, keepdims=True)
    scale = lax.rsqrt(jnp.mean(centred * centred, axis=-1, keepdims=True) + EPS)
    return centred * scale, scale


def normal_cdf(v):
    return 0.5 + 0.5 * lax.erf(v * 0.7071067811865476)


def gelu(v):
    return v * normal_cdf(v)


def kernel(
    comm,
    x1_hbm, x2_hbm, cot_hbm, wqkv_hbm, wout_hbm, wup_hbm, wdown_hbm,
    bias_hbm, p_last_hbm, p_side_hbm, p_inner_hbm, q_last_hbm, q_side_hbm, q_inner_hbm, gain_attn, gain_mlp,
    out, gi, gup_out, gdn_out,
    x2, cot, normed, normed_t, cot_t, back_norm, hid, bb,
    wqkv, wout, wup, wdown, bias, p_last, p_side, p_inner, q_last, q_side, q_inner, biases,
    g_up, g_dn, c_up, c_dn, h_up, h_dn, a1_up, a1_dn, u1, d1, a2_up, a2_dn, u2, d2, a3_up, a3_dn,
    x1, x1_side, row_in, corner_in, out_side, row_back, side_back, corner_back, tokens, padded, wqv_t, q_t, v_t, keys, att_t,
    load_sem, halo_send, halo_recv, back_send, back_recv,
    core_send, core_recv, s1_send, s1_recv, s2_send, s2_recv, s3_send, s3_recv,
):
    lat = lax.axis_index("lat")
    lon = lax.axis_index("lon")
    y_lo, z = lat // 4, lat % 4
    x, y_hi, core = lon // 4, (lon // 2) % 2, lon % 2
    y = y_hi * 2 + y_lo
    lat_next, lat_prev = (lat + 1) % 8, (lat + 7) % 8
    lon_next, lon_prev = (lon + 1) % 16, (lon + 15) % 16

    def core_peer():
        return (lat, lon + 1 - 2 * core)

    def x_peer(k):
        other = (x + k) % 4
        return other, (lat, other * 4 + y_hi * 2 + core)

    def z_peer(k):
        other = (z + k) % 4
        return other, (y_lo * 4 + other, lon)

    def y_peer(k):
        other = (y + k) % 4
        lo, hi = other % 2, other // 2
        return lo, hi, (lo * 4 + z, x * 4 + hi * 2 + core)

    def load(i, src, dst):
        return pltpu.make_async_copy(src, dst, load_sem.at[i])

    first_loads = [load(0, x2_hbm, x2), load(1, cot_hbm, cot)]

    def weight_loads(j):
        units = pl.ds(pl.multiple_of(j * CHUNK, CHUNK), CHUNK)
        return [
            load(2 + j, wup_hbm.at[:, units], wup.at[:, units]),
            load(2 + CHUNKS + j, wdown_hbm.at[units], wdown.at[units]),
        ]

    later_loads = [
        load(2 + 2 * CHUNKS + i, src, dst)
        for i, (src, dst) in enumerate((
            (x1_hbm, x1.at[pl.ds(0, ROWS)]), (wqkv_hbm, wqkv), (wout_hbm, wout),
            (p_last_hbm, p_last), (p_side_hbm, p_side), (p_inner_hbm, p_inner),
            (q_last_hbm, q_last), (q_side_hbm, q_side), (q_inner_hbm, q_inner),
        ))
    ]
    bias_load = load(11 + 2 * CHUNKS, bias_hbm, bias)
    for item in [bias_load] + first_loads + weight_loads(0):
        item.start()

    def remote(src, dst, send, recv, device):
        return pltpu.make_async_remote_copy(
            src_ref=src, dst_ref=dst, send_sem=send, recv_sem=recv,
            device_id=device, device_id_type=MESH,
        )

    halos = [
        remote(x1_hbm.at[pl.ds(0, SHIFT_H)], row_in, halo_send.at[0], halo_recv.at[0], (lat_prev, lon)),
        remote(
            x1_hbm.at[:, pl.ds(0, SIDE)], x1_side.at[pl.ds(0, ROWS)], halo_send.at[1], halo_recv.at[1],
            (lat, lon_prev),
        ),
        remote(
            x1_hbm.at[pl.ds(0, SHIFT_H), pl.ds(0, SIDE)], corner_in, halo_send.at[2], halo_recv.at[2],
            (lat_prev, lon_prev),
        ),
    ]
    if comm:
        barrier = pltpu.get_barrier_semaphore()
        peers = [
            (lat_next, lon), (lat_prev, lon), (lat, lon_next), (lat, lon_prev),
            (lat_next, lon_next), (lat_prev, lon_prev), core_peer(),
        ]
        for k in (2, 1, 3):
            peers += [x_peer(k)[1], z_peer(k)[1], y_peer(k)[2]]
        for peer in peers:
            pl.semaphore_signal(barrier, inc=1, device_id=peer, device_id_type=MESH)

    def meet():
        pl.semaphore_wait(barrier, len(peers))
        for item in (halos[1], halos[0], halos[2]):
            item.start()

    def core_copies(j):
        other = 1 - core
        return [
            remote(g_up.at[j, other], c_up.at[j], core_send.at[j, 0], core_recv.at[j, 0], core_peer()),
            remote(g_dn.at[j, other], c_dn.at[j], core_send.at[j, 1], core_recv.at[j, 1], core_peer()),
        ]

    def first_copies(j):
        copies = []
        for k in (2, 1, 3):
            other, device = z_peer(k)
            copies.append(remote(
                h_up.at[j, :, other], a1_up.at[k - 1, j], s1_send.at[j, k - 1, 0], s1_recv.at[j, k - 1, 0], device))
            other, device = x_peer(k)
            copies.append(remote(
                h_dn.at[j, :, other], a1_dn.at[k - 1, j], s1_send.at[j, k - 1, 1], s1_recv.at[j, k - 1, 1], device))
        return copies

    def second_copies():
        copies = []
        for k in (2, 1, 3):
            other, device = x_peer(k)
            copies.append(remote(
                u1.at[:, :, other], a2_up.at[k - 1], s2_send.at[k - 1, 0], s2_recv.at[k - 1, 0], device))
            other, device = z_peer(k)
            copies.append(remote(
                d1.at[:, other], a2_dn.at[k - 1], s2_send.at[k - 1, 1], s2_recv.at[k - 1, 1], device))
        return copies

    def third_copies():
        copies = []
        for k in (2, 1, 3):
            lo, hi, device = y_peer(k)
            copies.append(remote(
                u2.at[:, lo, hi], a3_up.at[k - 1], s3_send.at[k - 1, 0], s3_recv.at[k - 1, 0], device))
            copies.append(remote(
                d2.at[lo, hi], a3_dn.at[k - 1], s3_send.at[k - 1, 1], s3_recv.at[k - 1, 1], device))
        return copies

    def core_finish(j):
        if comm:
            for item in core_copies(j):
                item.wait()
        h_up[j] = (g_up[j, core].astype(F32) + c_up[j].astype(F32)).astype(BF16).reshape(2, 4, 8, 16, 128)
        h_dn[j] = (g_dn[j, core].astype(F32) + c_dn[j].astype(F32)).astype(BF16).reshape(2, 4, 2, 16, C)
        if comm:
            for item in first_copies(j):
                item.start()

    def first_finish():
        def wait_chunk(j, carry):
            for item in first_copies(j):
                item.wait()
            return carry

        if comm:
            lax.fori_loop(0, CHUNKS, wait_chunk, 0)
        total = h_up[:, :, z].astype(F32)
        for k in range(3):
            total += a1_up[k].astype(F32)
        u1[...] = total.astype(BF16).reshape(4, 2, 4, 2, 16, 128)
        total = h_dn[:, :, x].astype(F32)
        for k in range(3):
            total += a1_dn[k].astype(F32)
        d1[...] = total.astype(BF16).reshape(2, 4, 2, 16, C)
        if comm:
            for item in second_copies():
                item.start()

    def second_finish():
        if comm:
            for item in second_copies():
                item.wait()
        total = u1[:, :, x].astype(F32)
        for k in range(3):
            total += a2_up[k].astype(F32)
        u2[...] = total.astype(BF16)
        total = d1[:, z].astype(F32)
        for k in range(3):
            total += a2_dn[k].astype(F32)
        d2[...] = total.astype(BF16)
        if comm:
            for item in third_copies():
                item.start()

    def third_finish():
        if comm:
            for item in third_copies():
                item.wait()
        total = u2[:, y_lo, y_hi].astype(F32)
        for k in range(3):
            total += a3_up[k].astype(F32)
        for j in range(CHUNKS):
            for i in range(4):
                gup_out[:, CHUNK * j + 128 * i:CHUNK * j + 128 * (i + 1)] = total[j, 4 * i:4 * (i + 1)] * (1.0 / DEVICES)
        total = d2[y_lo, y_hi].astype(F32)
        for k in range(3):
            total += a3_dn[k].astype(F32)
        gdn_out[...] = total * (1.0 / DEVICES)

    bias_load.wait()
    upper_q = lax.broadcasted_iota(jnp.int32, (WINDOW, WINDOW), 0) < WINDOW // 2
    upper_k = lax.broadcasted_iota(jnp.int32, (WINDOW, WINDOW), 1) < WINDOW // 2
    split = jnp.where(upper_q == upper_k, 0.0, jnp.where(lat == 7, FAR, 0.0))
    biases[...] = jnp.zeros(biases.shape, F32)
    for head in range(HEADS):
        lanes = pl.ds(128 * (head % 2), WINDOW)
        turned = bias[head].T
        biases[0, head // 2, :, lanes] = turned
        biases[1, head // 2, :, lanes] = turned + split
    padded[...] = jnp.zeros(padded.shape, BF16)

    for item in first_loads:
        item.wait()
    for j in range(1, CHUNKS):
        for item in weight_loads(j):
            item.start()

    def prepare(t, carry):
        rows = pl.ds(pl.multiple_of(t * 384, 384), 384)
        band = pl.ds(t * 8, 8)
        centred, _ = normalize(x2[band].reshape(384, C).astype(F32))
        tile = (centred * gain_mlp[...]).astype(BF16)
        normed[rows, :] = tile
        normed_t[:, rows] = tile.T
        cot_t[:, rows] = cot[band].reshape(384, C).T
        return carry

    lax.fori_loop(0, 3, prepare, 0)

    sub = lax.broadcasted_iota(jnp.int32, (64, 8, 128), 1) < 4

    def chunk_step(j, carry):
        units = pl.ds(pl.multiple_of(j * CHUNK, CHUNK), CHUNK)
        for item in weight_loads(j):
            item.wait()

        @pl.when(j == 0)
        def _():
            for item in later_loads:
                item.start()

        w_in = wup[:, units]
        w_back = wdown[units, :]
        for t in range(2):
            rows = slice(t * HALF, (t + 1) * HALF)
            before = nn(normed[rows, :], w_in)
            back_hidden = nt(cot[12 * t:12 * (t + 1)].reshape(HALF, C), w_back)
            cdf = normal_cdf(before)
            hid[rows, :] = (before * cdf).astype(BF16)
            slope = cdf + before * (jnp.exp(before * before * -0.5) * 0.3989422804014327)
            back = (back_hidden * slope).astype(BF16)
            bb[rows, :] = back
            part = nt(back, w_in)
            back_norm[rows, :] = jnp.where(j == 0, part, back_norm[rows, :] + part)
        grad_up = nn(normed_t[...], bb[...])
        pieces = [grad_up[:, 128 * i:128 * (i + 1)].reshape(64, 8, 128) for i in range(4)]
        turned = [pltpu.roll(piece, 4, 1) for piece in pieces]
        for side in range(2):
            halves = []
            for i in (0, 2):
                if side == 0:
                    halves.append(jnp.where(sub, pieces[i], turned[i + 1]))
                else:
                    halves.append(jnp.where(sub, turned[i], pieces[i + 1]))
            g_up[j, side] = jnp.concatenate(halves, axis=1).astype(BF16)
        grad_down = nn(cot_t[...], hid[...]).astype(BF16).T.reshape(16, 2, 16, C)
        g_dn[j, 0] = grad_down[:, 0]
        g_dn[j, 1] = grad_down[:, 1]
        if comm:
            pl.when(j == 0)(meet)
            for item in core_copies(j):
                item.start()

        @pl.when(j >= 1)
        def _():
            core_finish(j - 1)

        return carry

    lax.fori_loop(0, CHUNKS, chunk_step, 0)

    def input_grad(t, carry):
        rows = pl.ds(pl.multiple_of(t * TILE, TILE), TILE)
        band = pl.ds(t * WH, WH)
        centred, scale = normalize(x2[band].reshape(TILE, C).astype(F32))
        back = back_norm[rows, :] * gain_mlp[...]
        mean_back = jnp.mean(back, axis=-1, keepdims=True)
        mean_both = jnp.mean(back * centred, axis=-1, keepdims=True)
        grad = cot[band].reshape(TILE, C).astype(F32) + scale * (back - mean_back - centred * mean_both)
        gi[band] = grad.astype(BF16).reshape(WH, COLS, C)
        return carry

    lax.fori_loop(0, TILES, input_grad, 0)
    core_finish(CHUNKS - 1)

    for item in later_loads:
        item.wait()
    if comm:
        for item in halos:
            item.wait()
    x1[ROWS:ROWS + SHIFT_H] = row_in[...]
    x1_side[ROWS:ROWS + SHIFT_H] = corner_in[...]
    wqv_t[0:C] = wqkv[:, 0:C].T
    wqv_t[C:2 * C] = wqkv[:, 2 * C:3 * C].T
    upper = lax.broadcasted_iota(jnp.int32, (128, 128), 0) < 64
    nothing = jnp.zeros((128, 128), BF16)
    gap = jnp.zeros((128 - WINDOW, 256), BF16)

    def project(windows):
        centred, _ = normalize(tokens[0:windows * WINDOW])
        centred = centred * gain_attn[...]
        for w in range(windows):
            padded[128 * w:128 * w + WINDOW] = centred[WINDOW * w:WINDOW * (w + 1)].astype(BF16)
        cells = padded[0:128 * windows]
        q_t[:, 0:128 * windows] = (nt(wqv_t[0:C], cells) * 0.125).astype(BF16)
        v_t[:, 0:128 * windows] = nt(wqv_t[C:2 * C], cells).astype(BF16)
        keys[0:128 * windows] = nn(cells, wqkv[:, C:2 * C]).astype(BF16)

    def attend(masks):
        def pair_step(pair, carry):
            heads = pl.ds(pl.multiple_of(pair * 128, 128), 128)
            scores, weights = [], []
            for w, masked in enumerate(masks):
                query = q_t[heads, w * 128:(w + 1) * 128]
                query = jnp.concatenate(
                    [jnp.where(upper, query, nothing), jnp.where(upper, nothing, query)], axis=1)
                scores.append(nn(keys[w * 128:w * 128 + WINDOW, heads], query) + biases[masked, pair])
            for score in scores:
                raised = jnp.exp(score - jnp.max(score, axis=0, keepdims=True))
                weights.append((raised.astype(BF16), 1.0 / jnp.sum(raised, axis=0, keepdims=True)))
            for w, (raised, inverse) in enumerate(weights):
                cells = slice(w * 128, (w + 1) * 128)
                blended = nn(v_t[heads, cells], jnp.concatenate([raised, gap], axis=0)) * inverse
                att_t[heads, cells] = jnp.where(upper, blended[:, :128], blended[:, 128:]).astype(BF16)
            return carry

        lax.fori_loop(0, HEADS // 2, pair_step, 0)

    def feed_forward(windows):
        mixed = lax.dot_general(
            att_t[:, 0:128 * windows], wout[...], (((0,), (0,)), ((), ())), preferred_element_type=F32)
        mixed = jnp.concatenate([mixed[128 * w:128 * w + WINDOW] for w in range(windows)], axis=0)
        residual = tokens[0:windows * WINDOW] + mixed
        mid, _ = normalize(residual)
        mid = (mid * gain_mlp[...]).astype(BF16)
        total = residual
        units = [slice(j * CHUNK, (j + 1) * CHUNK) for j in range(CHUNKS)]
        ready = nn(mid, wup[:, units[0]])
        for j in range(CHUNKS):
            coming = nn(mid, wup[:, units[j + 1]]) if j + 1 < CHUNKS else None
            hidden = gelu(ready).astype(BF16)
            total = total + nn(hidden, wdown[units[j], :])
            ready = coming
        return total

    above = pl.ds(SHIFT_H, INNER * WH)
    last = pl.ds(LAST, WH)
    tail = pl.ds(ROWS, SHIFT_H)
    right = pl.ds(COLS - SIDE, SIDE)
    cells = jnp.concatenate([x1[last].reshape(TILE, C), x1_side[last].reshape(WH * SIDE, C)], axis=0)
    tokens[0:TILE] = nn(p_last[...], cells)
    cells = jnp.concatenate(
        [x1[above, right].reshape(INNER * WH * SIDE, C), x1_side[above].reshape(INNER * WH * SIDE, C)], axis=0)
    tokens[TILE:EDGE * WINDOW] = nn(p_side[...], cells)[:INNER * WINDOW]
    project(EDGE)
    attend([1] * TILES + [0] * INNER)
    first_finish()
    total = feed_forward(EDGE)
    cells = nn(q_last[...], total[:TILE].astype(BF16)).astype(BF16)
    out[last] = cells[:TILE].reshape(WH, COLS, C)
    out_side[last] = cells[TILE:].reshape(WH, SIDE, C)
    cells = nn(q_side[...], total[TILE:].astype(BF16)).astype(BF16)
    out[above, right] = cells[:INNER * WH * SIDE].reshape(INNER * WH, SIDE, C)
    out_side[above] = cells[INNER * WH * SIDE:].reshape(INNER * WH, SIDE, C)
    inside = pl.ds(SHIFT_H, ROWS - SHIFT_H)
    returns = [
        remote(out.at[tail], row_back, back_send.at[0], back_recv.at[0], (lat_next, lon)),
        remote(out_side.at[inside], side_back.at[inside], back_send.at[1], back_recv.at[1], (lat, lon_next)),
        remote(out_side.at[tail], corner_back, back_send.at[2], back_recv.at[2], (lat_next, lon_next)),
    ]
    if comm:
        for item in (returns[1], returns[0], returns[2]):
            item.start()

    for b in range(INNER):
        band = pl.ds(SHIFT_H + WH * b, WH)
        rows = slice(INNER * WINDOW * b, INNER * WINDOW * (b + 1))
        tokens[rows] = nn(p_inner[...], x1[band].reshape(TILE, C))[:INNER * WINDOW]
    project(INNER * INNER)
    second_finish()
    attend([0] * (INNER * INNER))
    total = feed_forward(INNER * INNER)
    for b in range(INNER):
        band = pl.ds(SHIFT_H + WH * b, WH)
        rows = slice(INNER * WINDOW * b, INNER * WINDOW * (b + 1))
        cells = nn(q_inner[...], total[rows].astype(BF16)).astype(BF16).reshape(WH, COLS, C)
        out[band, pl.ds(0, COLS - SIDE)] = cells[:, :COLS - SIDE]
        out[band, right] = out[band, right] + cells[:, COLS - SIDE:]

    third_finish()
    if comm:
        for item in returns:
            item.wait()
    left = pl.ds(0, SIDE)
    out[inside, left] = out[inside, left] + side_back[inside]
    out[0:SHIFT_H] = row_back[...]
    out[0:SHIFT_H, left] = out[0:SHIFT_H, left] + corner_back[...]


def scratch():
    v = pltpu.VMEM
    tokens = ROWS * COLS
    ext = ROWS + SHIFT_H
    wide = INNER * INNER * 128
    dma = pltpu.SemaphoreType.DMA
    return [
        v((ROWS, COLS, C), BF16), v((ROWS, COLS, C), BF16), v((tokens, C), BF16), v((C, tokens), BF16),
        v((C, tokens), BF16), v((tokens, C), F32), v((tokens, CHUNK), BF16), v((tokens, CHUNK), BF16),
        v((C, 3 * C), BF16), v((C, C), BF16), v((C, FF), BF16), v((FF, C), BF16),
        v((HEADS, WINDOW, WINDOW), F32), *[v(place.shape, BF16) for place in window_orders()],
        v((2, HEADS // 2, WINDOW, 256), F32),
        v((CHUNKS, 2, 64, 16, 128), BF16), v((CHUNKS, 2, 16, 16, C), BF16),
        v((CHUNKS, 64, 16, 128), BF16), v((CHUNKS, 16, 16, C), BF16),
        v((CHUNKS, 2, 4, 8, 16, 128), BF16), v((CHUNKS, 2, 4, 2, 16, C), BF16),
        v((3, CHUNKS, 2, 8, 16, 128), BF16), v((3, CHUNKS, 2, 2, 16, C), BF16),
        v((CHUNKS, 2, 4, 2, 16, 128), BF16), v((2, 4, 2, 16, C), BF16),
        v((3, CHUNKS, 2, 2, 16, 128), BF16), v((3, 2, 2, 16, C), BF16),
        v((CHUNKS, 2, 2, 16, 128), BF16), v((2, 2, 16, C), BF16),
        v((3, CHUNKS, 16, 128), BF16), v((3, 16, C), BF16),
        v((ext, COLS, C), BF16), v((ext, SIDE, C), BF16), v((SHIFT_H, COLS, C), BF16),
        v((SHIFT_H, SIDE, C), BF16), v((ext, SIDE, C), BF16),
        v((SHIFT_H, COLS, C), BF16), v((ext, SIDE, C), BF16), v((SHIFT_H, SIDE, C), BF16),
        v((INNER * INNER * WINDOW, C), F32),
        v((wide, C), BF16), v((2 * C, C), BF16), v((C, wide), BF16), v((C, wide), BF16), v((wide, C), BF16), v((C, wide), BF16),
        dma((2 * CHUNKS + 12,)), dma((3,)), dma((3,)), dma((3,)), dma((3,)),
        dma((CHUNKS, 2)), dma((CHUNKS, 2)), dma((CHUNKS, 3, 2)), dma((CHUNKS, 3, 2)),
        dma((3, 2)), dma((3, 2)), dma((3, 2)), dma((3, 2)),
    ]


def place_results(first, grad, up, down, first_out, grad_out, up_out, down_out, sem):
    pairs = [(first.at[pl.ds(0, ROWS)], first_out), (grad, grad_out), (up, up_out), (down, down_out)]
    copies = [pltpu.make_async_copy(src, dst, sem.at[i]) for i, (src, dst) in enumerate(pairs)]
    for copy in copies:
        copy.start()
    for copy in copies:
        copy.wait()


def shards(comm, x_first, x_second, cotangent, gain_attn, gain_mlp, w_qkv, w_out, w_up, w_down, bias):
    places = window_orders()
    anywhere = pl.BlockSpec(memory_space=pl.ANY)
    near = pl.BlockSpec(memory_space=pltpu.VMEM)
    params = dict(vmem_limit_bytes=60 * 1024 * 1024, has_side_effects=True)
    if comm:
        params["collective_id"] = 0
    results = pl.pallas_call(
        functools.partial(kernel, comm),
        out_shape=(
            pltpu.VMEM((ROWS + SHIFT_H, COLS, C), BF16),
            pltpu.VMEM((ROWS, COLS, C), BF16),
            pltpu.VMEM((4, FF), F32),
            pltpu.VMEM((16, C), F32),
        ),
        in_specs=[anywhere] * 14 + [near] * 2,
        out_specs=(near,) * 4,
        scratch_shapes=scratch(),
        compiler_params=pltpu.CompilerParams(**params),
        cost_estimate=pl.CostEstimate(flops=20 * 10**9, bytes_accessed=13 * 10**6, transcendentals=10**7),
        name="swin_block",
    )(
        x_first, x_second, cotangent, w_qkv, w_out, w_up, w_down,
        bias, *[jnp.asarray(place, BF16) for place in places],
        gain_attn.reshape(1, C), gain_mlp.reshape(1, C),
    )
    return pl.pallas_call(
        place_results,
        out_shape=(
            jax.ShapeDtypeStruct((ROWS, COLS, C), BF16),
            jax.ShapeDtypeStruct((ROWS, COLS, C), BF16),
            jax.ShapeDtypeStruct((4, FF), F32),
            jax.ShapeDtypeStruct((16, C), F32),
        ),
        in_specs=[near] * 4,
        out_specs=(anywhere,) * 4,
        scratch_shapes=[pltpu.SemaphoreType.DMA((4,))],
        compiler_params=pltpu.CompilerParams(vmem_limit_bytes=1024 * 1024),
        name="place_results",
    )(*[pltpu.with_memory_space_constraint(item, pltpu.VMEM) for item in results])


def solution(mesh):
    cells = P("lat", "lon", None)
    return jax.shard_map(
        functools.partial(shards, True),
        mesh=mesh,
        in_specs=(cells, cells, cells) + (P(),) * 7,
        out_specs=(cells, cells, P(("lat", "lon"), None), P(("lat", "lon"), None)),
        check_vma=False,
    )
```
